256 devices in a mesh: blk: 32 (over y_hi, z, core), uly: 8 (over x, y_lo).
Axes of the slice: x: 4, y: 4 (y_hi: 2, y_lo: 2; y = y_hi * 2 + y_lo), z: 8, core: 2. Of those that a mesh axis runs over, the one named last changes fastest.
Arguments:
- query_in: bfloat16 [32768, 2048], P(('blk', 'uly')), may hold values from -6 to 6
- key_in: bfloat16 [32768, 2048], P(('blk', 'uly')), may hold values from -6 to 6
- value_in: bfloat16 [32768, 2048], P(('blk', 'uly')), may hold values from -6 to 6
- out_grad: bfloat16 [32768, 2048], P(('blk', 'uly')), may hold values from -6 to 6
Outputs:
- attended: bfloat16 [32768, 2048], P(('blk', 'uly'))
- grad_query: bfloat16 [32768, 2048], P(('blk', 'uly'))
- grad_key: bfloat16 [32768, 2048], P(('blk', 'uly'))
- grad_value: bfloat16 [32768, 2048], P(('blk', 'uly'))
The draws below stay inside these ranges and needn't reach their ends.
All inputs are finite; a program needn't handle non-finite values.
Results may differ from the reference program's by a relative error of at most 0.03.
Values may be sent and summed in bfloat16 or wider, within the bound.
A program may use at most 128 MiB of HBM per device.

```python
import jax
import jax.numpy as jnp
from jax import lax

HEADS = 16
HEAD_DIM = 128
BLOCK = 1024
TOKENS = 32768


def draw_query_in(key, part):
    key = jax.random.fold_in(key, 3)
    extent = (TOKENS, HEADS * HEAD_DIM)
    entries = jnp.clip(1.6 * jax.random.normal(key, extent, jnp.float32), -6.0, 6.0)
    return entries.astype(jnp.bfloat16)


def draw_key_in(key, part):
    key = jax.random.fold_in(key, 5)
    extent = (TOKENS, HEADS * HEAD_DIM)
    entries = jnp.clip(1.6 * jax.random.normal(key, extent, jnp.float32), -6.0, 6.0)
    return entries.astype(jnp.bfloat16)


def level_of(key, dims, pieces, smallest, largest):
    gain, own = 1.0, jax.random.fold_in(key, 6)
    for axis_at, parts in pieces:
        steps = jnp.exp(jax.random.uniform(jax.random.fold_in(own, axis_at), (parts,), jnp.float32, smallest / len(pieces), largest / len(pieces)))
        gain = gain * jnp.repeat(steps, dims[axis_at] // parts).reshape([-1 if axis == axis_at else 1 for axis in range(len(dims))])
    return gain


def scatter_about(key, shape, scale, most, pieces=(), kind=jnp.bfloat16):
    values = jax.random.normal(key, shape, jnp.float32) * scale
    if len(pieces) > 0:
        values = level_of(key, shape, pieces, -0.22, 0.18) * values
    return jnp.clip(values, min=-most, max=most).astype(kind)


def setup_inputs(seed: int = 0) -> dict:
    key_list = jax.random.split(jax.random.key(seed), 5)
    query_in = draw_query_in(jax.random.fold_in(key_list[4], 71), 0)
    key_in = draw_key_in(jax.random.fold_in(key_list[4], 71), 0)
    value_in = scatter_about(key_list[2], (TOKENS, HEADS * HEAD_DIM), 1.0, 6.0, ((0, 256),))
    out_grad = scatter_about(key_list[3], (TOKENS, HEADS * HEAD_DIM), 1.0, 6.0, ((0, 256),))
    return dict(query_in=query_in, key_in=key_in, value_in=value_in, out_grad=out_grad)


def one_head(query_head, key_head, value_head, grad_head):
    score_scale = HEAD_DIM ** -0.5
    blocks = TOKENS // BLOCK
    pad_rows = jnp.zeros((BLOCK, HEAD_DIM), jnp.bfloat16)
    key_padded = jnp.concatenate([pad_rows, key_head, pad_rows], axis=0)
    value_padded = jnp.concatenate([pad_rows, value_head, pad_rows], axis=0)
    width = 3 * BLOCK

    def step(carry, block_index):
        key_acc, value_acc = carry
        start = (block_index * BLOCK).astype(jnp.int32)
        query_blk = lax.dynamic_slice_in_dim(query_head, start, BLOCK, 0)
        grad_blk = lax.dynamic_slice_in_dim(grad_head, start, BLOCK, 0)
        key_blk = lax.dynamic_slice_in_dim(key_padded, start, width, 0)
        value_blk = lax.dynamic_slice_in_dim(value_padded, start, width, 0)
        owner = block_index - 1 + jnp.arange(width, dtype=jnp.int32) // BLOCK
        seen = jnp.logical_and(owner >= 0, owner < blocks)[None, :]
        scores = jnp.dot(query_blk, key_blk.T, preferred_element_type=jnp.float32) * score_scale
        scores = jnp.where(seen, scores, -jnp.inf)
        row_max = jnp.max(scores, axis=1, keepdims=True)
        log_norm = row_max + jnp.log(jnp.sum(jnp.exp(scores - row_max), axis=1, keepdims=True))
        probas = jnp.exp(scores - log_norm)
        weights = probas.astype(jnp.bfloat16)
        attended = jnp.dot(weights, value_blk, preferred_element_type=jnp.float32).astype(jnp.bfloat16)
        row_dot = jnp.sum(grad_blk.astype(jnp.float32) * attended.astype(jnp.float32), axis=1, keepdims=True)
        value_term = jnp.dot(weights.T, grad_blk, preferred_element_type=jnp.float32)
        grad_probs = jnp.dot(grad_blk, value_blk.T, preferred_element_type=jnp.float32)
        grad_scores = (probas * (grad_probs - row_dot)).astype(jnp.bfloat16)
        query_grad = (jnp.dot(grad_scores, key_blk, preferred_element_type=jnp.float32) * score_scale).astype(jnp.bfloat16)
        key_term = jnp.dot(grad_scores.T, query_blk, preferred_element_type=jnp.float32)
        key_acc = lax.dynamic_update_slice_in_dim(
            key_acc, lax.dynamic_slice_in_dim(key_acc, start, width, 0) + key_term, start, 0)
        value_acc = lax.dynamic_update_slice_in_dim(
            value_acc, lax.dynamic_slice_in_dim(value_acc, start, width, 0) + value_term, start, 0)
        return (key_acc, value_acc), (attended, query_grad)

    empty = jnp.zeros((TOKENS + 2 * BLOCK, HEAD_DIM), jnp.float32)
    (key_acc, value_acc), (attended, query_grad) = lax.scan(
        step, (empty, empty), jnp.arange(blocks, dtype=jnp.int32))
    grad_key = (key_acc[BLOCK:BLOCK + TOKENS] * score_scale).astype(jnp.bfloat16)
    grad_value = value_acc[BLOCK:BLOCK + TOKENS].astype(jnp.bfloat16)
    return (attended.reshape(TOKENS, HEAD_DIM), query_grad.reshape(TOKENS, HEAD_DIM), grad_key, grad_value)


def split_heads(matrix):
    return matrix.reshape(TOKENS, HEADS, HEAD_DIM).transpose(1, 0, 2)


def join_heads(stacked):
    return stacked.transpose(1, 0, 2).reshape(TOKENS, HEADS * HEAD_DIM)


def reference(query_in, key_in, value_in, out_grad):
    results = lax.map(lambda group: one_head(group[0], group[1], group[2], group[3]),
                      (split_heads(query_in), split_heads(key_in), split_heads(value_in), split_heads(out_grad)))
    return (join_heads(results[0]), join_heads(results[1]), join_heads(results[2]), join_heads(results[3]))
```

```python
import jax
import jax.numpy as jnp
from jax import lax
from jax.experimental import pallas as pl
from jax.experimental.pallas import tpu as pltpu
from jax.sharding import PartitionSpec as P

HEADS = 16
HEAD_DIM = 128
SCALE = HEAD_DIM ** (-0.5)
LOG2_SCALE = SCALE * 1.4426950408889634
MESH = pl.DeviceIdType.MESH
CHUNK = 512
Q, K, V, G = range(4)
O, DQ, DK, DV = range(4)


def dot(a, b):
    return jnp.dot(a, b, preferred_element_type=jnp.float32)


def kernel(
    q_in, k_in, v_in, g_in, o_out, dq_out, dk_out, dv_out,
    q_buf, g_buf, k_buf, v_buf, scores, weights, o_buf, dq_buf, dk_buf, dv_buf,
    own_dk, own_dv, edge_out, edge_in,
    in_send, in_recv, halo_send, halo_recv, edge_send, edge_recv, out_send, out_recv,
):
    rows = q_in.shape[0]
    block = q_buf.shape[1]
    blocks = lax.axis_size("blk")
    width = lax.axis_size("uly")
    place = lax.axis_index("blk")
    member = lax.axis_index("uly")
    has_left = place > 0
    has_right = place < blocks - 1
    column_x, column_y = lax.div(member, 2), lax.rem(member, 2)
    inputs, outputs = (q_in, k_in, v_in, g_in), (o_out, dq_out, dk_out, dv_out)

    def peer(r):
        x = lax.rem(column_x + lax.div(r, 2), width // 2)
        y = lax.rem(column_y + lax.rem(r, 2), 2)
        return x * 2 + y

    def each_peer(body):
        lax.fori_loop(1, width, lambda r, _: (body(jnp.int32(r)), 0)[1], 0)

    barrier = pltpu.get_barrier_semaphore()
    each_peer(
        lambda r: pl.semaphore_signal(
            barrier, inc=1, device_id=(place, peer(r)), device_id_type=MESH
        )
    )

    @pl.when(has_left)
    def _():
        pl.semaphore_signal(barrier, inc=1, device_id=(place - 1, member), device_id_type=MESH)

    @pl.when(has_right)
    def _():
        pl.semaphore_signal(barrier, inc=1, device_id=(place + 1, member), device_id_type=MESH)

    pl.semaphore_wait(
        barrier, width - 1 + has_left.astype(jnp.int32) + has_right.astype(jnp.int32)
    )

    def columns(owner, h):
        return pl.ds(pl.multiple_of((owner * 2 + h) * HEAD_DIM, HEAD_DIM), HEAD_DIM)

    def token_rows(owner):
        return pl.ds(pl.multiple_of(owner * rows, rows), rows)

    def in_place(a, h):
        if a == Q:
            return q_buf.at[h, token_rows(member)]
        if a == G:
            return g_buf.at[h, token_rows(member)]
        buf = k_buf if a == K else v_buf
        return buf.at[h, 1, token_rows(member)]

    def in_copy(a, h, r):
        return pltpu.make_async_remote_copy(
            src_ref=inputs[a].at[:, columns(peer(r), h)],
            dst_ref=in_place(a, h),
            send_sem=in_send.at[a, h, r],
            recv_sem=in_recv.at[a, h, r],
            device_id=(place, peer(r)),
            device_id_type=MESH,
        )

    def in_own(a, h):
        return pltpu.make_async_copy(
            inputs[a].at[:, columns(member, h)], in_place(a, h), in_recv.at[a, h, 0]
        )

    def send_in(a, h):
        each_peer(lambda r: in_copy(a, h, r).start())
        in_own(a, h).start()

    def wait_in(a, h):
        each_peer(lambda r: in_copy(a, h, r).wait_recv())
        in_own(a, h).wait()

    def pair_copies(src, dst, send, recv):
        right = pltpu.make_async_remote_copy(
            src_ref=src[0], dst_ref=dst[0], send_sem=send[0], recv_sem=recv[0],
            device_id=(place + 1, member), device_id_type=MESH,
        )
        left = pltpu.make_async_remote_copy(
            src_ref=src[1], dst_ref=dst[1], send_sem=send[1], recv_sem=recv[1],
            device_id=(place - 1, member), device_id_type=MESH,
        )
        return right, left

    def halo(a, h):
        buf, i = (k_buf, 0) if a == K else (v_buf, 1)
        own = buf.at[h, 1]
        return pair_copies(
            (own, own), (buf.at[h, 0], buf.at[h, 2]),
            (halo_send.at[i, h, 0], halo_send.at[i, h, 1]),
            (halo_recv.at[i, h, 0], halo_recv.at[i, h, 1]),
        )

    def edge(i, h):
        return pair_copies(
            (edge_out.at[i, h, 0], edge_out.at[i, h, 1]),
            (edge_in.at[i, h, 0], edge_in.at[i, h, 1]),
            (edge_send.at[i, h, 0], edge_send.at[i, h, 1]),
            (edge_recv.at[i, h, 0], edge_recv.at[i, h, 1]),
        )

    def start_pair(pair):
        right, left = pair
        pl.when(has_right)(right.start)
        pl.when(has_left)(left.start)

    def wait_recv_pair(pair):
        right, left = pair
        pl.when(has_left)(right.wait_recv)
        pl.when(has_right)(left.wait_recv)

    def wait_send_pair(pair):
        right, left = pair
        pl.when(has_right)(right.wait_send)
        pl.when(has_left)(left.wait_send)

    results = (o_buf, dq_buf, dk_buf, dv_buf)

    def out_copy(i, h, r):
        return pltpu.make_async_remote_copy(
            src_ref=results[i].at[h, token_rows(peer(r))],
            dst_ref=outputs[i].at[:, columns(member, h)],
            send_sem=out_send.at[i, h, r],
            recv_sem=out_recv.at[i, h, r],
            device_id=(place, peer(r)),
            device_id_type=MESH,
        )

    def out_own(i, h):
        return pltpu.make_async_copy(
            results[i].at[h, token_rows(member)],
            outputs[i].at[:, columns(member, h)],
            out_recv.at[i, h, 0],
        )

    def send_out(i, h):
        each_peer(lambda r: out_copy(i, h, r).start())
        out_own(i, h).start()

    for a in (K, Q, V, G):
        send_in(a, 0)

    @pl.when(jnp.logical_not(has_left))
    def _():
        k_buf[:, 0] = jnp.zeros_like(k_buf[:, 0])
        v_buf[:, 0] = jnp.zeros_like(v_buf[:, 0])
        edge_in[:, :, 0] = jnp.zeros_like(edge_in[:, :, 0])

    @pl.when(jnp.logical_not(has_right))
    def _():
        k_buf[:, 2] = jnp.zeros_like(k_buf[:, 2])
        v_buf[:, 2] = jnp.zeros_like(v_buf[:, 2])
        edge_in[:, :, 1] = jnp.zeros_like(edge_in[:, :, 1])

    seen = (has_left, None, has_right)
    per_slot = block // CHUNK

    def piece(c):
        return slice(c * CHUNK, (c + 1) * CHUNK)

    def slot_scores(h, slot, query_t):
        best = jnp.full((8, block), -jnp.inf, jnp.float32)
        for c in range(per_slot):
            part = dot(k_buf[h, slot, piece(c)], query_t)
            scores[slot, piece(c)] = part
            best = jnp.maximum(best, jnp.max(part.reshape(CHUNK // 8, 8, block), axis=0))
        if seen[slot] is not None:
            best = jnp.where(seen[slot], best, -jnp.inf)
        return best

    def slot_weights(h, slot, top):
        if seen[slot] is not None:
            top = jnp.where(seen[slot], top, jnp.float32(1e30))
        total = jnp.zeros((8, block), jnp.float32)
        acc = jnp.zeros((HEAD_DIM, block), jnp.float32)
        for c in range(per_slot):
            raised = jnp.exp2(scores[slot, piece(c)] * LOG2_SCALE - top)
            total = total + jnp.sum(raised.reshape(CHUNK // 8, 8, block), axis=0)
            low = raised.astype(jnp.bfloat16)
            weights[slot, piece(c)] = low
            acc = acc + dot(v_buf[h, slot, piece(c)].T, low)
        return total, acc

    def slot_grads(h, slot, query, grad, grad_t, row_dot, dk_ref, dv_ref):
        acc = jnp.zeros((HEAD_DIM, block), jnp.float32)
        for c in range(per_slot):
            low = weights[slot, piece(c)]
            grad_probs = dot(v_buf[h, slot, piece(c)], grad_t)
            grad_scores = (low.astype(jnp.float32) * (grad_probs - row_dot)).astype(jnp.bfloat16)
            dv_ref[piece(c)] = dot(low, grad).astype(dv_ref.dtype)
            dk_ref[piece(c)] = dot(grad_scores, query).astype(dk_ref.dtype)
            acc = acc + dot(k_buf[h, slot, piece(c)].T, grad_scores)
        return acc

    def finish_keys(h):
        for i, (own, buf, scale) in enumerate(((own_dk, dk_buf, SCALE), (own_dv, dv_buf, 1.0))):
            wait_recv_pair(edge(i, h))
            total = (
                own[h]
                + edge_in[i, h, 0].astype(jnp.float32)
                + edge_in[i, h, 1].astype(jnp.float32)
            )
            buf[h] = (total * scale).astype(jnp.bfloat16)
            send_out(DK + i, h)

    for h in range(2):
        if h == 0:
            wait_in(K, 0)
            start_pair(halo(K, 0))
            send_in(K, 1)
        wait_in(Q, h)
        query = q_buf[h]
        query_t = query.T
        best = slot_scores(h, 1, query_t)
        if h == 0:
            wait_in(V, 0)
            start_pair(halo(V, 0))
            send_in(Q, 1)
            send_in(V, 1)
            send_in(G, 1)
        wait_recv_pair(halo(K, h))
        for slot in (0, 2):
            best = jnp.maximum(best, slot_scores(h, slot, query_t))
        if h == 1:
            finish_keys(0)
        wait_recv_pair(halo(V, h))
        top = jnp.max(best, axis=0, keepdims=True) * LOG2_SCALE
        total, acc = slot_weights(h, 1, top)
        for slot in (0, 2):
            more, term = slot_weights(h, slot, top)
            total, acc = total + more, acc + term
        inverse = 1.0 / jnp.sum(total, axis=0, keepdims=True)
        attended_t = (acc * inverse).astype(jnp.bfloat16)
        o_buf[h] = attended_t.T
        send_out(O, h)
        if h == 0:
            wait_in(K, 1)
            start_pair(halo(K, 1))
        wait_in(G, h)
        grad_t = (g_buf[h].T.astype(jnp.float32) * inverse).astype(jnp.bfloat16)
        row_dot = jnp.sum(
            grad_t.astype(jnp.float32) * attended_t.astype(jnp.float32), axis=0, keepdims=True
        )
        grad = grad_t.T
        acc = slot_grads(
            h, 2, query, grad, grad_t, row_dot, edge_out.at[0, h, 0], edge_out.at[1, h, 0]
        )
        acc = acc + slot_grads(
            h, 0, query, grad, grad_t, row_dot, edge_out.at[0, h, 1], edge_out.at[1, h, 1]
        )
        start_pair(edge(0, h))
        start_pair(edge(1, h))
        if h == 0:
            wait_in(V, 1)
            start_pair(halo(V, 1))
        acc = acc + slot_grads(h, 1, query, grad, grad_t, row_dot, own_dk.at[h], own_dv.at[h])
        dq_buf[h] = (acc * SCALE).astype(jnp.bfloat16).T
        send_out(DQ, h)
    finish_keys(1)

    for h in range(2):
        for a in range(4):
            each_peer(lambda r: in_copy(a, h, r).wait_send())
        for i in range(2):
            wait_send_pair(halo((K, V)[i], h))
            wait_send_pair(edge(i, h))
        for i in range(4):
            each_peer(lambda r: out_copy(i, h, r).wait())
            out_own(i, h).wait()


def local(query_in, key_in, value_in, out_grad):
    width = lax.axis_size("uly")
    rows, _ = query_in.shape
    block = rows * width
    heads = HEADS // width
    low, full = jnp.bfloat16, jnp.float32
    dma = pltpu.SemaphoreType.DMA
    whole = pl.BlockSpec(memory_space=pl.ANY)
    return pl.pallas_call(
        kernel,
        in_specs=[whole] * 4,
        out_specs=[whole] * 4,
        out_shape=[jax.ShapeDtypeStruct(query_in.shape, low)] * 4,
        scratch_shapes=[
            pltpu.VMEM((heads, block, HEAD_DIM), low),
            pltpu.VMEM((heads, block, HEAD_DIM), low),
            pltpu.VMEM((heads, 3, block, HEAD_DIM), low),
            pltpu.VMEM((heads, 3, block, HEAD_DIM), low),
            pltpu.VMEM((3, block, block), full),
            pltpu.VMEM((3, block, block), low),
            pltpu.VMEM((heads, block, HEAD_DIM), low),
            pltpu.VMEM((heads, block, HEAD_DIM), low),
            pltpu.VMEM((heads, block, HEAD_DIM), low),
            pltpu.VMEM((heads, block, HEAD_DIM), low),
            pltpu.VMEM((heads, block, HEAD_DIM), full),
            pltpu.VMEM((heads, block, HEAD_DIM), full),
            pltpu.VMEM((2, heads, 2, block, HEAD_DIM), low),
            pltpu.VMEM((2, heads, 2, block, HEAD_DIM), low),
            dma((4, heads, width)),
            dma((4, heads, width)),
            dma((2, heads, 2)),
            dma((2, heads, 2)),
            dma((2, heads, 2)),
            dma((2, heads, 2)),
            dma((4, heads, width)),
            dma((4, heads, width)),
        ],
        compiler_params=pltpu.CompilerParams(
            collective_id=0, has_side_effects=True, vmem_limit_bytes=60 * 2**20
        ),
        cost_estimate=pl.CostEstimate(
            flops=12 * heads * 3 * block * block * HEAD_DIM,
            bytes_accessed=16 * rows * HEADS * HEAD_DIM,
            transcendentals=heads * 3 * block * block,
        ),
    )(query_in, key_in, value_in, out_grad)


def solution(mesh):
    spec = P(("blk", "uly"), None)
    return jax.shard_map(
        local,
        mesh=mesh,
        in_specs=(spec,) * 4,
        out_specs=(spec,) * 4,
        check_vma=False,
    )
```

```python
import jax
import jax.numpy as jnp
from jax import lax
from jax.experimental import pallas as pl
from jax.experimental.pallas import tpu as pltpu
from jax.sharding import PartitionSpec as P

HEADS = 16
HEAD_DIM = 128
SCALE = HEAD_DIM ** (-0.5)
LOG2_SCALE = SCALE * 1.4426950408889634
MESH = pl.DeviceIdType.MESH
CHUNK = 512
Q, K, V, G = range(4)
O, DQ, DK, DV = range(4)


def dot(a, b):
    return jnp.dot(a, b, preferred_element_type=jnp.float32)


def kernel(
    q_in, k_in, v_in, g_in, o_out, dq_out, dk_out, dv_out,
    q_buf, g_buf, k_buf, v_buf, scores, weights, o_buf, dq_buf, dk_buf, dv_buf,
    own_dk, own_dv, edge_out, edge_in,
    in_send, in_recv, halo_send, halo_recv, edge_send, edge_recv, out_send, out_recv,
):
    rows = q_in.shape[0]
    block = q_buf.shape[1]
    blocks = lax.axis_size("blk")
    width = lax.axis_size("uly")
    place = lax.axis_index("blk")
    member = lax.axis_index("uly")
    has_left = place > 0
    has_right = place < blocks - 1
    column_x, column_y = lax.div(member, 2), lax.rem(member, 2)
    inputs, outputs = (q_in, k_in, v_in, g_in), (o_out, dq_out, dk_out, dv_out)

    def peer(r):
        x = lax.rem(column_x + lax.div(r, 2), width // 2)
        y = lax.rem(column_y + lax.rem(r, 2), 2)
        return x * 2 + y

    def flipped(owner):
        return owner + 1 - 2 * lax.rem(owner, 2)

    upper = place >= blocks // 2

    def heads_of(owner):
        return jnp.where(upper, flipped(owner), owner)

    right = (place + 1, jnp.where(place == blocks // 2 - 1, flipped(member), member))
    left = (place - 1, jnp.where(place == blocks // 2, flipped(member), member))

    def each_peer(body):
        lax.fori_loop(1, width, lambda r, _: (body(jnp.int32(r)), 0)[1], 0)

    barrier = pltpu.get_barrier_semaphore()
    each_peer(
        lambda r: pl.semaphore_signal(
            barrier, inc=1, device_id=(place, peer(r)), device_id_type=MESH
        )
    )

    @pl.when(has_left)
    def _():
        pl.semaphore_signal(barrier, inc=1, device_id=left, device_id_type=MESH)

    @pl.when(has_right)
    def _():
        pl.semaphore_signal(barrier, inc=1, device_id=right, device_id_type=MESH)

    pl.semaphore_wait(
        barrier, width - 1 + has_left.astype(jnp.int32) + has_right.astype(jnp.int32)
    )

    def columns(owner, h):
        return pl.ds(pl.multiple_of((heads_of(owner) * 2 + h) * HEAD_DIM, HEAD_DIM), HEAD_DIM)

    def token_rows(owner):
        return pl.ds(pl.multiple_of(owner * rows, rows), rows)

    def in_place(a, h):
        if a == Q:
            return q_buf.at[h, token_rows(member)]
        if a == G:
            return g_buf.at[h, token_rows(member)]
        buf = k_buf if a == K else v_buf
        return buf.at[h, 1, token_rows(member)]

    def in_copy(a, h, r):
        return pltpu.make_async_remote_copy(
            src_ref=inputs[a].at[:, columns(peer(r), h)],
            dst_ref=in_place(a, h),
            send_sem=in_send.at[a, h, r],
            recv_sem=in_recv.at[a, h, r],
            device_id=(place, peer(r)),
            device_id_type=MESH,
        )

    def in_own(a, h):
        return pltpu.make_async_copy(
            inputs[a].at[:, columns(member, h)], in_place(a, h), in_recv.at[a, h, 0]
        )

    def send_in(a, h):
        each_peer(lambda r: in_copy(a, h, r).start())
        in_own(a, h).start()

    def wait_in(a, h):
        each_peer(lambda r: in_copy(a, h, r).wait_recv())
        in_own(a, h).wait()

    def pair_copies(src, dst, send, recv):
        to_right = pltpu.make_async_remote_copy(
            src_ref=src[0], dst_ref=dst[0], send_sem=send[0], recv_sem=recv[0],
            device_id=right, device_id_type=MESH,
        )
        to_left = pltpu.make_async_remote_copy(
            src_ref=src[1], dst_ref=dst[1], send_sem=send[1], recv_sem=recv[1],
            device_id=left, device_id_type=MESH,
        )
        return to_right, to_left

    def halo(a, h):
        buf, i = (k_buf, 0) if a == K else (v_buf, 1)
        own = buf.at[h, 1]
        return pair_copies(
            (own, own), (buf.at[h, 0], buf.at[h, 2]),
            (halo_send.at[i, h, 0], halo_send.at[i, h, 1]),
            (halo_recv.at[i, h, 0], halo_recv.at[i, h, 1]),
        )

    def edge(i, h):
        return pair_copies(
            (edge_out.at[i, h, 0], edge_out.at[i, h, 1]),
            (edge_in.at[i, h, 0], edge_in.at[i, h, 1]),
            (edge_send.at[i, h, 0], edge_send.at[i, h, 1]),
            (edge_recv.at[i, h, 0], edge_recv.at[i, h, 1]),
        )

    def start_pair(pair):
        to_right, to_left = pair
        pl.when(has_right)(to_right.start)
        pl.when(has_left)(to_left.start)

    def wait_recv_pair(pair):
        to_right, to_left = pair
        pl.when(has_left)(to_right.wait_recv)
        pl.when(has_right)(to_left.wait_recv)

    def wait_send_pair(pair):
        to_right, to_left = pair
        pl.when(has_right)(to_right.wait_send)
        pl.when(has_left)(to_left.wait_send)

    results = (o_buf, dq_buf, dk_buf, dv_buf)

    def out_copy(i, h, r):
        return pltpu.make_async_remote_copy(
            src_ref=results[i].at[h, token_rows(peer(r))],
            dst_ref=outputs[i].at[:, columns(member, h)],
            send_sem=out_send.at[i, h, r],
            recv_sem=out_recv.at[i, h, r],
            device_id=(place, peer(r)),
            device_id_type=MESH,
        )

    def out_own(i, h):
        return pltpu.make_async_copy(
            results[i].at[h, token_rows(member)],
            outputs[i].at[:, columns(member, h)],
            out_recv.at[i, h, 0],
        )

    def send_out(i, h):
        each_peer(lambda r: out_copy(i, h, r).start())
        out_own(i, h).start()

    for a in (K, Q, V, G):
        send_in(a, 0)

    @pl.when(jnp.logical_not(has_left))
    def _():
        k_buf[:, 0] = jnp.zeros_like(k_buf[:, 0])
        v_buf[:, 0] = jnp.zeros_like(v_buf[:, 0])
        edge_in[:, :, 0] = jnp.zeros_like(edge_in[:, :, 0])

    @pl.when(jnp.logical_not(has_right))
    def _():
        k_buf[:, 2] = jnp.zeros_like(k_buf[:, 2])
        v_buf[:, 2] = jnp.zeros_like(v_buf[:, 2])
        edge_in[:, :, 1] = jnp.zeros_like(edge_in[:, :, 1])

    seen = (has_left, None, has_right)
    per_slot = block // CHUNK

    def piece(c):
        return slice(c * CHUNK, (c + 1) * CHUNK)

    def slot_scores(h, slot, query_t):
        best = jnp.full((8, block), -jnp.inf, jnp.float32)
        for c in range(per_slot):
            part = dot(k_buf[h, slot, piece(c)], query_t)
            scores[slot, piece(c)] = part
            best = jnp.maximum(best, jnp.max(part.reshape(CHUNK // 8, 8, block), axis=0))
        if seen[slot] is not None:
            best = jnp.where(seen[slot], best, -jnp.inf)
        return best

    def slot_weights(h, slot, top):
        if seen[slot] is not None:
            top = jnp.where(seen[slot], top, jnp.float32(1e30))
        total = jnp.zeros((8, block), jnp.float32)
        acc = jnp.zeros((HEAD_DIM, block), jnp.float32)
        for c in range(per_slot):
            raised = jnp.exp2(scores[slot, piece(c)] * LOG2_SCALE - top)
            total = total + jnp.sum(raised.reshape(CHUNK // 8, 8, block), axis=0)
            low = raised.astype(jnp.bfloat16)
            weights[slot, piece(c)] = low
            acc = acc + dot(v_buf[h, slot, piece(c)].T, low)
        return total, acc

    def slot_grads(h, slot, query, grad, grad_t, row_dot, dk_ref, dv_ref):
        acc = jnp.zeros((HEAD_DIM, block), jnp.float32)
        for c in range(per_slot):
            low = weights[slot, piece(c)]
            grad_probs = dot(v_buf[h, slot, piece(c)], grad_t)
            grad_scores = (low.astype(jnp.float32) * (grad_probs - row_dot)).astype(jnp.bfloat16)
            dv_ref[piece(c)] = dot(low, grad).astype(dv_ref.dtype)
            dk_ref[piece(c)] = dot(grad_scores, query).astype(dk_ref.dtype)
            acc = acc + dot(k_buf[h, slot, piece(c)].T, grad_scores)
        return acc

    def finish_keys(h):
        for i, (own, buf, scale) in enumerate(((own_dk, dk_buf, SCALE), (own_dv, dv_buf, 1.0))):
            wait_recv_pair(edge(i, h))
            total = (
                own[h]
                + edge_in[i, h, 0].astype(jnp.float32)
                + edge_in[i, h, 1].astype(jnp.float32)
            )
            buf[h] = (total * scale).astype(jnp.bfloat16)
            send_out(DK + i, h)

    for h in range(2):
        if h == 0:
            wait_in(K, 0)
            start_pair(halo(K, 0))
            send_in(K, 1)
        wait_in(Q, h)
        query = q_buf[h]
        query_t = query.T
        best = slot_scores(h, 1, query_t)
        if h == 0:
            wait_in(V, 0)
            start_pair(halo(V, 0))
            send_in(Q, 1)
            send_in(V, 1)
            send_in(G, 1)
        wait_recv_pair(halo(K, h))
        for slot in (0, 2):
            best = jnp.maximum(best, slot_scores(h, slot, query_t))
        if h == 1:
            finish_keys(0)
        wait_recv_pair(halo(V, h))
        top = jnp.max(best, axis=0, keepdims=True) * LOG2_SCALE
        total, acc = slot_weights(h, 1, top)
        for slot in (0, 2):
            more, term = slot_weights(h, slot, top)
            total, acc = total + more, acc + term
        inverse = 1.0 / jnp.sum(total, axis=0, keepdims=True)
        attended_t = (acc * inverse).astype(jnp.bfloat16)
        o_buf[h] = attended_t.T
        send_out(O, h)
        if h == 0:
            wait_in(K, 1)
            start_pair(halo(K, 1))
        wait_in(G, h)
        grad_t = (g_buf[h].T.astype(jnp.float32) * inverse).astype(jnp.bfloat16)
        row_dot = jnp.sum(
            grad_t.astype(jnp.float32) * attended_t.astype(jnp.float32), axis=0, keepdims=True
        )
        grad = grad_t.T
        acc = slot_grads(
            h, 2, query, grad, grad_t, row_dot, edge_out.at[0, h, 0], edge_out.at[1, h, 0]
        )
        acc = acc + slot_grads(
            h, 0, query, grad, grad_t, row_dot, edge_out.at[0, h, 1], edge_out.at[1, h, 1]
        )
        start_pair(edge(0, h))
        start_pair(edge(1, h))
        if h == 0:
            wait_in(V, 1)
            start_pair(halo(V, 1))
        acc = acc + slot_grads(h, 1, query, grad, grad_t, row_dot, own_dk.at[h], own_dv.at[h])
        dq_buf[h] = (acc * SCALE).astype(jnp.bfloat16).T
        send_out(DQ, h)
    finish_keys(1)

    for h in range(2):
        for a in range(4):
            each_peer(lambda r: in_copy(a, h, r).wait_send())
        for i in range(2):
            wait_send_pair(halo((K, V)[i], h))
            wait_send_pair(edge(i, h))
        for i in range(4):
            each_peer(lambda r: out_copy(i, h, r).wait())
            out_own(i, h).wait()


def hand_over(*refs):
    sources, targets, (held, fetched, stored) = refs[:4], refs[4:8], refs[8:]
    fetch = [pltpu.make_async_copy(sources[i], held.at[i], fetched.at[i]) for i in range(4)]
    store = [pltpu.make_async_copy(held.at[i], targets[i], stored.at[i]) for i in range(4)]
    for copy in fetch:
        copy.start()
    for i in range(4):
        fetch[i].wait()
        store[i].start()
    for copy in store:
        copy.wait()


def local(query_in, key_in, value_in, out_grad):
    width = lax.axis_size("uly")
    rows, _ = query_in.shape
    block = rows * width
    heads = HEADS // width
    low, full = jnp.bfloat16, jnp.float32
    dma = pltpu.SemaphoreType.DMA
    whole = pl.BlockSpec(memory_space=pl.ANY)
    results = pl.pallas_call(
        kernel,
        in_specs=[whole] * 4,
        out_specs=[whole] * 4,
        out_shape=[jax.ShapeDtypeStruct(query_in.shape, low)] * 4,
        scratch_shapes=[
            pltpu.VMEM((heads, block, HEAD_DIM), low),
            pltpu.VMEM((heads, block, HEAD_DIM), low),
            pltpu.VMEM((heads, 3, block, HEAD_DIM), low),
            pltpu.VMEM((heads, 3, block, HEAD_DIM), low),
            pltpu.VMEM((3, block, block), full),
            pltpu.VMEM((3, block, block), low),
            pltpu.VMEM((heads, block, HEAD_DIM), low),
            pltpu.VMEM((heads, block, HEAD_DIM), low),
            pltpu.VMEM((heads, block, HEAD_DIM), low),
            pltpu.VMEM((heads, block, HEAD_DIM), low),
            pltpu.VMEM((heads, block, HEAD_DIM), full),
            pltpu.VMEM((heads, block, HEAD_DIM), full),
            pltpu.VMEM((2, heads, 2, block, HEAD_DIM), low),
            pltpu.VMEM((2, heads, 2, block, HEAD_DIM), low),
            dma((4, heads, width)),
            dma((4, heads, width)),
            dma((2, heads, 2)),
            dma((2, heads, 2)),
            dma((2, heads, 2)),
            dma((2, heads, 2)),
            dma((4, heads, width)),
            dma((4, heads, width)),
        ],
        compiler_params=pltpu.CompilerParams(
            collective_id=0, has_side_effects=True, vmem_limit_bytes=60 * 2**20
        ),
        cost_estimate=pl.CostEstimate(
            flops=12 * heads * 3 * block * block * HEAD_DIM,
            bytes_accessed=16 * rows * HEADS * HEAD_DIM,
            transcendentals=heads * 3 * block * block,
        ),
    )(query_in, key_in, value_in, out_grad)
    return pl.pallas_call(
        hand_over,
        in_specs=[whole] * 4,
        out_specs=[whole] * 4,
        out_shape=[jax.ShapeDtypeStruct(query_in.shape, low)] * 4,
        scratch_shapes=[pltpu.VMEM((4, *query_in.shape), low), dma((4,)), dma((4,))],
    )(*results)


def solution(mesh):
    spec = P(("blk", "uly"), None)
    return jax.shard_map(
        local,
        mesh=mesh,
        in_specs=(spec,) * 4,
        out_specs=(spec,) * 4,
        check_vma=False,
    )
```

```python
import jax
import jax.numpy as jnp
from jax import lax
from jax.experimental import pallas as pl
from jax.experimental.pallas import tpu as pltpu
from jax.sharding import PartitionSpec as P

HEADS = 16
HEAD_DIM = 128
SCALE = HEAD_DIM ** (-0.5)
LOG2_SCALE = SCALE * 1.4426950408889634
MESH = pl.DeviceIdType.MESH
CHUNK = 512
Q, K, V, G = range(4)
O, DQ, DK, DV = range(4)
FAR, CORE, OWN = range(3)


def dot(a, b):
    return jnp.dot(a, b, preferred_element_type=jnp.float32)


def kernel(
    q_in, k_in, v_in, g_in, o_out, dq_out, dk_out, dv_out,
    q_buf, g_buf, k_buf, v_buf, scores, weights, o_buf, dq_buf, dk_buf, dv_buf,
    own_dk, own_dv, edge_out, edge_in,
    in_send, in_recv, halo_send, halo_recv, edge_send, edge_recv, out_send, out_recv,
):
    rows = q_in.shape[0]
    block = q_buf.shape[1]
    blocks = lax.axis_size("blk")
    width = lax.axis_size("uly")
    place = lax.axis_index("blk")
    member = lax.axis_index("uly")
    core = lax.rem(place, 2)
    column_x, column_y = lax.div(member, 2), lax.rem(member, 2)
    inputs, outputs = (q_in, k_in, v_in, g_in), (o_out, dq_out, dk_out, dv_out)

    def peer(r):
        x = lax.rem(column_x + lax.div(r, 2), width // 2)
        y = lax.rem(column_y + lax.rem(r, 2), 2)
        return x * 2 + y

    def flipped(owner):
        return owner + 1 - 2 * lax.rem(owner, 2)

    upper = place >= blocks // 2

    def heads_of(owner):
        return jnp.where(upper, flipped(owner), owner)

    far = place + 2 * core - 1
    has_far = jnp.logical_and(far >= 0, far < blocks)
    crosses = jnp.logical_or(
        jnp.logical_and(place == blocks // 2 - 1, core == 1),
        jnp.logical_and(place == blocks // 2, core == 0),
    )
    sides = (
        (far, jnp.where(crosses, flipped(member), member)),
        (place + 1 - 2 * core, member),
    )

    def each_peer(body):
        lax.fori_loop(1, width, lambda r, _: (body(jnp.int32(r)), 0)[1], 0)

    barrier = pltpu.get_barrier_semaphore()
    each_peer(
        lambda r: pl.semaphore_signal(
            barrier, inc=1, device_id=(place, peer(r)), device_id_type=MESH
        )
    )
    pl.semaphore_signal(barrier, inc=1, device_id=sides[CORE], device_id_type=MESH)

    @pl.when(has_far)
    def _():
        pl.semaphore_signal(barrier, inc=1, device_id=sides[FAR], device_id_type=MESH)

    pl.semaphore_wait(barrier, width + has_far.astype(jnp.int32))

    def columns(owner, h):
        return pl.ds(pl.multiple_of((heads_of(owner) * 2 + h) * HEAD_DIM, HEAD_DIM), HEAD_DIM)

    def token_rows(owner):
        return pl.ds(pl.multiple_of(owner * rows, rows), rows)

    def in_place(a, h):
        if a == Q:
            return q_buf.at[h, token_rows(member)]
        if a == G:
            return g_buf.at[h, token_rows(member)]
        buf = k_buf if a == K else v_buf
        return buf.at[h, OWN, token_rows(member)]

    def in_copy(a, h, r):
        return pltpu.make_async_remote_copy(
            src_ref=inputs[a].at[:, columns(peer(r), h)],
            dst_ref=in_place(a, h),
            send_sem=in_send.at[a, h, r],
            recv_sem=in_recv.at[a, h, r],
            device_id=(place, peer(r)),
            device_id_type=MESH,
        )

    def in_own(a, h):
        return pltpu.make_async_copy(
            inputs[a].at[:, columns(member, h)], in_place(a, h), in_recv.at[a, h, 0]
        )

    def send_in(a, h):
        each_peer(lambda r: in_copy(a, h, r).start())
        in_own(a, h).start()

    def wait_in(a, h):
        each_peer(lambda r: in_copy(a, h, r).wait_recv())
        in_own(a, h).wait()

    def halo(a, h, side):
        buf, i = (k_buf, 0) if a == K else (v_buf, 1)
        return pltpu.make_async_remote_copy(
            src_ref=buf.at[h, OWN],
            dst_ref=buf.at[h, side],
            send_sem=halo_send.at[i, h, side],
            recv_sem=halo_recv.at[i, h, side],
            device_id=sides[side],
            device_id_type=MESH,
        )

    def edge(i, h, side):
        return pltpu.make_async_remote_copy(
            src_ref=edge_out.at[i, h, side],
            dst_ref=edge_in.at[i, h, side],
            send_sem=edge_send.at[i, h, side],
            recv_sem=edge_recv.at[i, h, side],
            device_id=sides[side],
            device_id_type=MESH,
        )

    def if_there(side, action):
        if side == FAR:
            pl.when(has_far)(action)
        else:
            action()

    def start_halo(a, h):
        for side in (FAR, CORE):
            if_there(side, halo(a, h, side).start)

    def start_edges(h, side):
        for i in range(2):
            if_there(side, edge(i, h, side).start)

    results = (o_buf, dq_buf, dk_buf, dv_buf)

    def out_copy(i, h, r):
        return pltpu.make_async_remote_copy(
            src_ref=results[i].at[h, token_rows(peer(r))],
            dst_ref=outputs[i].at[:, columns(member, h)],
            send_sem=out_send.at[i, h, r],
            recv_sem=out_recv.at[i, h, r],
            device_id=(place, peer(r)),
            device_id_type=MESH,
        )

    def out_own(i, h):
        return pltpu.make_async_copy(
            results[i].at[h, token_rows(member)],
            outputs[i].at[:, columns(member, h)],
            out_recv.at[i, h, 0],
        )

    def send_out(i, h):
        each_peer(lambda r: out_copy(i, h, r).start())
        out_own(i, h).start()

    for h in range(2):
        for a in (K, V, Q, G):
            send_in(a, h)

    @pl.when(jnp.logical_not(has_far))
    def _():
        k_buf[:, FAR] = jnp.zeros_like(k_buf[:, FAR])
        v_buf[:, FAR] = jnp.zeros_like(v_buf[:, FAR])
        edge_in[:, :, FAR] = jnp.zeros_like(edge_in[:, :, FAR])

    per_slot = block // CHUNK

    def piece(c):
        return slice(c * CHUNK, (c + 1) * CHUNK)

    def slot_scores(h, slot, query_t):
        best = jnp.full((8, block), -jnp.inf, jnp.float32)
        for c in range(per_slot):
            part = dot(k_buf[h, slot, piece(c)], query_t)
            scores[slot, piece(c)] = part
            best = jnp.maximum(best, jnp.max(part.reshape(CHUNK // 8, 8, block), axis=0))
        if slot == FAR:
            best = jnp.where(has_far, best, -jnp.inf)
        return best

    def slot_weights(h, slot, top):
        if slot == FAR:
            top = jnp.where(has_far, top, jnp.float32(1e30))
        total = jnp.zeros((8, block), jnp.float32)
        acc = jnp.zeros((HEAD_DIM, block), jnp.float32)
        for c in range(per_slot):
            raised = jnp.exp2(scores[slot, piece(c)] * LOG2_SCALE - top)
            total = total + jnp.sum(raised.reshape(CHUNK // 8, 8, block), axis=0)
            low = raised.astype(jnp.bfloat16)
            weights[slot, piece(c)] = low
            acc = acc + dot(v_buf[h, slot, piece(c)].T, low)
        return total, acc

    def slot_grads(h, slot, query, grad, grad_t, row_dot, dk_ref, dv_ref):
        acc = jnp.zeros((HEAD_DIM, block), jnp.float32)
        for c in range(per_slot):
            low = weights[slot, piece(c)]
            grad_probs = dot(v_buf[h, slot, piece(c)], grad_t)
            grad_scores = (low.astype(jnp.float32) * (grad_probs - row_dot)).astype(jnp.bfloat16)
            dv_ref[piece(c)] = dot(low, grad).astype(dv_ref.dtype)
            dk_ref[piece(c)] = dot(grad_scores, query).astype(dk_ref.dtype)
            acc = acc + dot(k_buf[h, slot, piece(c)].T, grad_scores)
        return acc

    def finish_keys(h):
        for i, (own, buf, scale) in enumerate(((own_dk, dk_buf, SCALE), (own_dv, dv_buf, 1.0))):
            for side in (CORE, FAR):
                if_there(side, edge(i, h, side).wait_recv)
            total = (
                own[h]
                + edge_in[i, h, 0].astype(jnp.float32)
                + edge_in[i, h, 1].astype(jnp.float32)
            )
            buf[h] = (total * scale).astype(jnp.bfloat16)
            send_out(DK + i, h)

    def forward(a, h):
        wait_in(a, h)
        start_halo(a, h)

    def wait_halo(a, h, side):
        if_there(side, halo(a, h, side).wait_recv)

    forward(K, 0)
    forward(V, 0)
    for h in range(2):
        wait_in(Q, h)
        query = q_buf[h]
        query_t = query.T
        best = slot_scores(h, OWN, query_t)
        for slot in (CORE, FAR):
            wait_halo(K, h, slot)
            best = jnp.maximum(best, slot_scores(h, slot, query_t))
        top = jnp.max(best, axis=0, keepdims=True) * LOG2_SCALE
        total, acc = slot_weights(h, OWN, top)
        for slot in (CORE, FAR):
            wait_halo(V, h, slot)
            more, term = slot_weights(h, slot, top)
            total, acc = total + more, acc + term
        inverse = 1.0 / jnp.sum(total, axis=0, keepdims=True)
        attended_t = (acc * inverse).astype(jnp.bfloat16)
        o_buf[h] = attended_t.T
        send_out(O, h)
        if h == 0:
            forward(K, 1)
        else:
            finish_keys(0)
        wait_in(G, h)
        grad_t = (g_buf[h].T.astype(jnp.float32) * inverse).astype(jnp.bfloat16)
        row_dot = jnp.sum(
            grad_t.astype(jnp.float32) * attended_t.astype(jnp.float32), axis=0, keepdims=True
        )
        grad = grad_t.T
        acc = slot_grads(
            h, FAR, query, grad, grad_t, row_dot, edge_out.at[0, h, FAR], edge_out.at[1, h, FAR]
        )
        if h == 0:
            forward(V, 1)
        start_edges(h, FAR)
        acc = acc + slot_grads(
            h, CORE, query, grad, grad_t, row_dot, edge_out.at[0, h, CORE], edge_out.at[1, h, CORE]
        )
        start_edges(h, CORE)
        acc = acc + slot_grads(h, OWN, query, grad, grad_t, row_dot, own_dk.at[h], own_dv.at[h])
        dq_buf[h] = (acc * SCALE).astype(jnp.bfloat16).T
        send_out(DQ, h)
    for h in range(2):
        for a in range(4):
            each_peer(lambda r: in_copy(a, h, r).wait_send())
        for side in (FAR, CORE):
            for a in (K, V):
                if_there(side, halo(a, h, side).wait_send)
    finish_keys(1)

    for h in range(2):
        for side in (FAR, CORE):
            for i in range(2):
                if_there(side, edge(i, h, side).wait_send)
        for i in range(4):
            each_peer(lambda r: out_copy(i, h, r).wait())
            out_own(i, h).wait()


def hand_over(*refs):
    sources, targets, (held, fetched, stored) = refs[:4], refs[4:8], refs[8:]
    count = fetched.shape[1]
    rows = held.shape[1] // count
    pieces = [(i, j, pl.ds(j * rows, rows)) for i in range(4) for j in range(count)]
    fetch = [
        pltpu.make_async_copy(sources[i].at[part], held.at[i, part], fetched.at[i, j])
        for i, j, part in pieces
    ]
    store = [
        pltpu.make_async_copy(held.at[i, part], targets[i].at[part], stored.at[i, j])
        for i, j, part in pieces
    ]
    for copy in fetch:
        copy.start()
    for before, after in zip(fetch, store):
        before.wait()
        after.start()
    for copy in store:
        copy.wait()


def local(query_in, key_in, value_in, out_grad):
    width = lax.axis_size("uly")
    rows, _ = query_in.shape
    block = rows * width
    heads = HEADS // width
    low, full = jnp.bfloat16, jnp.float32
    dma = pltpu.SemaphoreType.DMA
    whole = pl.BlockSpec(memory_space=pl.ANY)
    results = pl.pallas_call(
        kernel,
        in_specs=[whole] * 4,
        out_specs=[whole] * 4,
        out_shape=[jax.ShapeDtypeStruct(query_in.shape, low)] * 4,
        scratch_shapes=[
            pltpu.VMEM((heads, block, HEAD_DIM), low),
            pltpu.VMEM((heads, block, HEAD_DIM), low),
            pltpu.VMEM((heads, 3, block, HEAD_DIM), low),
            pltpu.VMEM((heads, 3, block, HEAD_DIM), low),
            pltpu.VMEM((3, block, block), full),
            pltpu.VMEM((3, block, block), low),
            pltpu.VMEM((heads, block, HEAD_DIM), low),
            pltpu.VMEM((heads, block, HEAD_DIM), low),
            pltpu.VMEM((heads, block, HEAD_DIM), low),
            pltpu.VMEM((heads, block, HEAD_DIM), low),
            pltpu.VMEM((heads, block, HEAD_DIM), full),
            pltpu.VMEM((heads, block, HEAD_DIM), full),
            pltpu.VMEM((2, heads, 2, block, HEAD_DIM), low),
            pltpu.VMEM((2, heads, 2, block, HEAD_DIM), low),
            dma((4, heads, width)),
            dma((4, heads, width)),
            dma((2, heads, 2)),
            dma((2, heads, 2)),
            dma((2, heads, 2)),
            dma((2, heads, 2)),
            dma((4, heads, width)),
            dma((4, heads, width)),
        ],
        compiler_params=pltpu.CompilerParams(
            collective_id=0, has_side_effects=True, vmem_limit_bytes=60 * 2**20
        ),
        cost_estimate=pl.CostEstimate(
            flops=12 * heads * 3 * block * block * HEAD_DIM,
            bytes_accessed=16 * rows * HEADS * HEAD_DIM,
            transcendentals=heads * 3 * block * block,
        ),
    )(query_in, key_in, value_in, out_grad)
    return pl.pallas_call(
        hand_over,
        in_specs=[whole] * 4,
        out_specs=[whole] * 4,
        out_shape=[jax.ShapeDtypeStruct(query_in.shape, low)] * 4,
        scratch_shapes=[pltpu.VMEM((4, *query_in.shape), low), dma((4, 4)), dma((4, 4))],
    )(*results)


def solution(mesh):
    spec = P(("blk", "uly"), None)
    return jax.shard_map(
        local,
        mesh=mesh,
        in_specs=(spec,) * 4,
        out_specs=(spec,) * 4,
        check_vma=False,
    )
```

```python
import jax
import jax.numpy as jnp
from jax import lax
from jax.experimental import pallas as pl
from jax.experimental.pallas import tpu as pltpu
from jax.sharding import PartitionSpec as P

HEADS = 16
HEAD_DIM = 128
SCALE = HEAD_DIM ** (-0.5)
LOG2_SCALE = SCALE * 1.4426950408889634
MESH = pl.DeviceIdType.MESH
CHUNK = 512
Q, K, V, G = range(4)
O, DQ, DK, DV = range(4)
FAR, CORE, OWN = range(3)


def dot(a, b):
    return jnp.dot(a, b, preferred_element_type=jnp.float32)


def kernel(
    q_in, k_in, v_in, g_in, o_out, dq_out, dk_out, dv_out,
    q_buf, g_buf, k_buf, v_buf, scores, weights, o_buf, dq_buf, dk_buf, dv_buf,
    own_dk, own_dv, edge_out, edge_in,
    in_send, in_recv, halo_send, halo_recv, edge_send, edge_recv, out_send, out_recv,
):
    rows = q_in.shape[0]
    block = q_buf.shape[1]
    blocks = lax.axis_size("blk")
    width = lax.axis_size("uly")
    place = lax.axis_index("blk")
    member = lax.axis_index("uly")
    core = lax.rem(place, 2)
    column_x, column_y = lax.div(member, 2), lax.rem(member, 2)
    inputs, outputs = (q_in, k_in, v_in, g_in), (o_out, dq_out, dk_out, dv_out)

    def peer(r):
        x = lax.rem(column_x + lax.div(r, 2), width // 2)
        y = lax.rem(column_y + lax.rem(r, 2), 2)
        return x * 2 + y

    def flipped(owner):
        return owner + 1 - 2 * lax.rem(owner, 2)

    upper = place >= blocks // 2

    def heads_of(owner):
        return jnp.where(upper, flipped(owner), owner)

    far = place + 2 * core - 1
    has_far = jnp.logical_and(far >= 0, far < blocks)
    crosses = jnp.logical_or(
        jnp.logical_and(place == blocks // 2 - 1, core == 1),
        jnp.logical_and(place == blocks // 2, core == 0),
    )
    sides = (
        (far, jnp.where(crosses, flipped(member), member)),
        (place + 1 - 2 * core, member),
    )

    def each_peer(body):
        lax.fori_loop(1, width, lambda r, _: (body(jnp.int32(r)), 0)[1], 0)

    barrier = pltpu.get_barrier_semaphore()
    each_peer(
        lambda r: pl.semaphore_signal(
            barrier, inc=1, device_id=(place, peer(r)), device_id_type=MESH
        )
    )
    pl.semaphore_signal(barrier, inc=1, device_id=sides[CORE], device_id_type=MESH)

    @pl.when(has_far)
    def _():
        pl.semaphore_signal(barrier, inc=1, device_id=sides[FAR], device_id_type=MESH)

    pl.semaphore_wait(barrier, width + has_far.astype(jnp.int32))

    per_slot = block // CHUNK

    def piece(c):
        return slice(c * CHUNK, (c + 1) * CHUNK)

    def columns(owner, h):
        return pl.ds(pl.multiple_of((heads_of(owner) * 2 + h) * HEAD_DIM, HEAD_DIM), HEAD_DIM)

    def token_rows(owner):
        return pl.ds(pl.multiple_of(owner * rows, rows), rows)

    def landing(a, h):
        if a == Q:
            return q_buf.at[h]
        if a == G:
            return g_buf.at[h]
        return (k_buf if a == K else v_buf).at[h, OWN]

    def in_place(a, h):
        return landing(a, h).at[token_rows(member)]

    def wait_bytes(ref, sem):
        pltpu.make_async_copy(ref, ref, sem).wait()

    def in_copy(a, h, r):
        return pltpu.make_async_remote_copy(
            src_ref=inputs[a].at[:, columns(peer(r), h)],
            dst_ref=in_place(a, h),
            send_sem=in_send.at[a],
            recv_sem=in_recv.at[a, h],
            device_id=(place, peer(r)),
            device_id_type=MESH,
        )

    def in_own(a, h):
        return pltpu.make_async_copy(
            inputs[a].at[:, columns(member, h)], in_place(a, h), in_recv.at[a, h]
        )

    def send_in(a, h):
        each_peer(lambda r: in_copy(a, h, r).start())
        in_own(a, h).start()

    def wait_in(a, h):
        wait_bytes(landing(a, h), in_recv.at[a, h])

    def halo(a, h, side):
        buf, i = (k_buf, 0) if a == K else (v_buf, 1)
        return pltpu.make_async_remote_copy(
            src_ref=buf.at[h, OWN],
            dst_ref=buf.at[h, side],
            send_sem=halo_send.at[i, side],
            recv_sem=halo_recv.at[i, h, side],
            device_id=sides[side],
            device_id_type=MESH,
        )

    def edge(i, h, side, c):
        return pltpu.make_async_remote_copy(
            src_ref=edge_out.at[i, h, side, pl.ds(c * CHUNK, CHUNK)],
            dst_ref=edge_in.at[i, h, side, pl.ds(c * CHUNK, CHUNK)],
            send_sem=edge_send.at[i, side],
            recv_sem=edge_recv.at[i, h, side],
            device_id=sides[side],
            device_id_type=MESH,
        )

    def if_there(side, action):
        if side == FAR:
            pl.when(has_far)(action)
        else:
            action()

    def start_halo(a, h):
        for side in (FAR, CORE):
            if_there(side, halo(a, h, side).start)

    results = (o_buf, dq_buf, dk_buf, dv_buf)

    def out_copy(i, h, r):
        return pltpu.make_async_remote_copy(
            src_ref=results[i].at[h, token_rows(peer(r))],
            dst_ref=outputs[i].at[:, columns(member, h)],
            send_sem=out_send.at[i],
            recv_sem=out_recv.at[i],
            device_id=(place, peer(r)),
            device_id_type=MESH,
        )

    def out_own(i, h):
        return pltpu.make_async_copy(
            results[i].at[h, token_rows(member)],
            outputs[i].at[:, columns(member, h)],
            out_recv.at[i],
        )

    def send_out(i, h):
        each_peer(lambda r: out_copy(i, h, r).start())
        out_own(i, h).start()

    for a, h in ((K, 0), (V, 0), (Q, 0), (K, 1), (G, 0), (V, 1), (Q, 1), (G, 1)):
        send_in(a, h)

    @pl.when(jnp.logical_not(has_far))
    def _():
        k_buf[:, FAR] = jnp.zeros_like(k_buf[:, FAR])
        v_buf[:, FAR] = jnp.zeros_like(v_buf[:, FAR])
        edge_in[:, :, FAR] = jnp.zeros_like(edge_in[:, :, FAR])

    def slot_scores(h, slot, query_t):
        best = jnp.full((8, block), -jnp.inf, jnp.float32)
        for c in range(per_slot):
            part = dot(k_buf[h, slot, piece(c)], query_t)
            scores[slot, piece(c)] = part
            best = jnp.maximum(best, jnp.max(part.reshape(CHUNK // 8, 8, block), axis=0))
        if slot == FAR:
            best = jnp.where(has_far, best, -jnp.inf)
        return best

    def slot_weights(h, slot, top):
        if slot == FAR:
            top = jnp.where(has_far, top, jnp.float32(1e30))
        total = jnp.zeros((8, block), jnp.float32)
        acc = jnp.zeros((HEAD_DIM, block), jnp.float32)
        for c in range(per_slot):
            raised = jnp.exp2(scores[slot, piece(c)] * LOG2_SCALE - top)
            total = total + jnp.sum(raised.reshape(CHUNK // 8, 8, block), axis=0)
            low = raised.astype(jnp.bfloat16)
            weights[slot, piece(c)] = low
            acc = acc + dot(v_buf[h, slot, piece(c)].T, low)
        return total, acc

    def slot_grads(h, slot, query, grad, grad_t, row_dot, dk_ref, dv_ref):
        acc = jnp.zeros((HEAD_DIM, block), jnp.float32)
        for c in range(per_slot):
            low = weights[slot, piece(c)]
            grad_probs = dot(v_buf[h, slot, piece(c)], grad_t)
            grad_scores = (low.astype(jnp.float32) * (grad_probs - row_dot)).astype(jnp.bfloat16)
            dv_ref[piece(c)] = dot(low, grad).astype(dv_ref.dtype)
            dk_ref[piece(c)] = dot(grad_scores, query).astype(dk_ref.dtype)
            if slot != OWN:
                for i in range(2):
                    if_there(slot, edge(i, h, slot, c).start)
            acc = acc + dot(k_buf[h, slot, piece(c)].T, grad_scores)
        return acc

    def finish_keys(h):
        for i, (own, buf, scale) in enumerate(((own_dk, dk_buf, SCALE), (own_dv, dv_buf, 1.0))):
            for side in (CORE, FAR):
                if_there(
                    side, lambda: wait_bytes(edge_in.at[i, h, side], edge_recv.at[i, h, side])
                )
            total = (
                own[h]
                + edge_in[i, h, 0].astype(jnp.float32)
                + edge_in[i, h, 1].astype(jnp.float32)
            )
            buf[h] = (total * scale).astype(jnp.bfloat16)
            send_out(DK + i, h)

    def forward(a, h):
        wait_in(a, h)
        start_halo(a, h)

    def wait_halo(a, h, side):
        if_there(side, halo(a, h, side).wait_recv)

    forward(K, 0)
    forward(V, 0)
    for h in range(2):
        wait_in(Q, h)
        query = q_buf[h]
        query_t = query.T
        best = slot_scores(h, OWN, query_t)
        for slot in (CORE, FAR):
            wait_halo(K, h, slot)
            best = jnp.maximum(best, slot_scores(h, slot, query_t))
        top = jnp.max(best, axis=0, keepdims=True) * LOG2_SCALE
        total, acc = slot_weights(h, OWN, top)
        for slot in (CORE, FAR):
            if h == 0 and slot == FAR:
                forward(K, 1)
            wait_halo(V, h, slot)
            more, term = slot_weights(h, slot, top)
            total, acc = total + more, acc + term
        inverse = 1.0 / jnp.sum(total, axis=0, keepdims=True)
        attended_t = (acc * inverse).astype(jnp.bfloat16)
        o_buf[h] = attended_t.T
        send_out(O, h)
        wait_in(G, h)
        grad_t = (g_buf[h].T.astype(jnp.float32) * inverse).astype(jnp.bfloat16)
        row_dot = jnp.sum(
            grad_t.astype(jnp.float32) * attended_t.astype(jnp.float32), axis=0, keepdims=True
        )
        grad = grad_t.T
        acc = None
        for slot in (CORE, FAR) if h == 0 else (FAR, CORE):
            term = slot_grads(
                h, slot, query, grad, grad_t, row_dot, edge_out.at[0, h, slot], edge_out.at[1, h, slot]
            )
            if acc is None:
                acc = term
                if h == 0:
                    forward(V, 1)
                else:
                    finish_keys(0)
            else:
                acc = acc + term
        acc = acc + slot_grads(h, OWN, query, grad, grad_t, row_dot, own_dk.at[h], own_dv.at[h])
        dq_buf[h] = (acc * SCALE).astype(jnp.bfloat16).T
        send_out(DQ, h)
    others = pl.ds(0, (width - 1) * rows)
    for a, buf in ((Q, q_buf), (G, g_buf)):
        wait_bytes(buf.at[:, others], in_send.at[a])
    for i, buf in enumerate((k_buf, v_buf)):
        wait_bytes(buf.at[:, OWN, others], in_send.at[(K, V)[i]])
        for side in (FAR, CORE):
            if_there(side, lambda: wait_bytes(buf.at[:, side], halo_send.at[i, side]))
    finish_keys(1)

    for i in range(2):
        for side in (FAR, CORE):
            if_there(side, lambda: wait_bytes(edge_out.at[i, :, side], edge_send.at[i, side]))
    for i in range(4):
        wait_bytes(results[i].at[:, others], out_send.at[i])
        wait_bytes(outputs[i], out_recv.at[i])


def hand_over(*refs):
    sources, targets, done = refs[:4], refs[4:8], refs[8]
    count = done.shape[1]
    rows = sources[0].shape[0] // count
    copies = [
        pltpu.make_async_copy(
            sources[i].at[pl.ds(j * rows, rows)], targets[i].at[pl.ds(j * rows, rows)], done.at[i, j]
        )
        for i in range(4)
        for j in range(count)
    ]
    for copy in copies:
        copy.start()
    for copy in copies:
        copy.wait()


def local(query_in, key_in, value_in, out_grad):
    width = lax.axis_size("uly")
    rows, _ = query_in.shape
    block = rows * width
    heads = HEADS // width
    low, full = jnp.bfloat16, jnp.float32
    dma = pltpu.SemaphoreType.DMA
    whole = pl.BlockSpec(memory_space=pl.ANY)
    query_in, key_in, value_in, out_grad = (
        pltpu.with_memory_space_constraint(array, pltpu.HBM)
        for array in (query_in, key_in, value_in, out_grad)
    )
    results = pl.pallas_call(
        kernel,
        in_specs=[whole] * 4,
        out_specs=[whole] * 4,
        out_shape=[pltpu.VMEM(query_in.shape, low)] * 4,
        scratch_shapes=[
            pltpu.VMEM((heads, block, HEAD_DIM), low),
            pltpu.VMEM((heads, block, HEAD_DIM), low),
            pltpu.VMEM((heads, 3, block, HEAD_DIM), low),
            pltpu.VMEM((heads, 3, block, HEAD_DIM), low),
            pltpu.VMEM((3, block, block), full),
            pltpu.VMEM((3, block, block), low),
            pltpu.VMEM((heads, block, HEAD_DIM), low),
            pltpu.VMEM((heads, block, HEAD_DIM), low),
            pltpu.VMEM((heads, block, HEAD_DIM), low),
            pltpu.VMEM((heads, block, HEAD_DIM), low),
            pltpu.VMEM((heads, block, HEAD_DIM), full),
            pltpu.VMEM((heads, block, HEAD_DIM), full),
            pltpu.VMEM((2, heads, 2, block, HEAD_DIM), low),
            pltpu.VMEM((2, heads, 2, block, HEAD_DIM), low),
            dma((4,)),
            dma((4, heads)),
            dma((2, 2)),
            dma((2, heads, 2)),
            dma((2, 2)),
            dma((2, heads, 2)),
            dma((4,)),
            dma((4,)),
        ],
        compiler_params=pltpu.CompilerParams(
            collective_id=0, has_side_effects=True, vmem_limit_bytes=44 * 2**20
        ),
        cost_estimate=pl.CostEstimate(
            flops=12 * heads * 3 * block * block * HEAD_DIM,
            bytes_accessed=16 * rows * HEADS * HEAD_DIM,
            transcendentals=heads * 3 * block * block,
        ),
    )(query_in, key_in, value_in, out_grad)
    return pl.pallas_call(
        hand_over,
        in_specs=[whole] * 4,
        out_specs=[whole] * 4,
        out_shape=[jax.ShapeDtypeStruct(query_in.shape, low)] * 4,
        scratch_shapes=[dma((4, 4))],
    )(*(pltpu.with_memory_space_constraint(result, pltpu.VMEM) for result in results))


def solution(mesh):
    spec = P(("blk", "uly"), None)
    return jax.shard_map(
        local,
        mesh=mesh,
        in_specs=(spec,) * 4,
        out_specs=(spec,) * 4,
        check_vma=False,
    )
```

```python
import jax
import jax.numpy as jnp
from jax import lax
from jax.experimental import pallas as pl
from jax.experimental.pallas import tpu as pltpu
from jax.sharding import PartitionSpec as P

HEADS = 16
HEAD_DIM = 128
SCALE = HEAD_DIM ** (-0.5)
LOG2_SCALE = SCALE * 1.4426950408889634
MESH = pl.DeviceIdType.MESH
CHUNK = 512
Q, K, V, G = range(4)
O, DQ, DK, DV = range(4)
FAR, CORE, OWN = range(3)
FAR_FIRST = 0o6214735


def dot(a, b):
    return jnp.dot(a, b, preferred_element_type=jnp.float32)


def kernel(
    q_in, k_in, v_in, g_in, o_out, dq_out, dk_out, dv_out,
    q_buf, g_buf, k_buf, v_buf, scores, weights, o_buf, dq_buf, dk_buf, dv_buf,
    own_dk, own_dv, edge_out, edge_in,
    in_send, in_recv, halo_send, halo_recv, edge_send, edge_recv, out_send, out_recv, near,
):
    rows = q_in.shape[0]
    block = q_buf.shape[1]
    blocks = lax.axis_size("blk")
    width = lax.axis_size("uly")
    place = lax.axis_index("blk")
    member = lax.axis_index("uly")
    core = lax.rem(place, 2)
    column_x, column_y = lax.div(member, 2), lax.rem(member, 2)
    inputs, outputs = (q_in, k_in, v_in, g_in), (o_out, dq_out, dk_out, dv_out)

    def peer(r):
        x = lax.rem(column_x + lax.div(r, 2), width // 2)
        y = lax.rem(column_y + lax.rem(r, 2), 2)
        return x * 2 + y

    def flipped(owner):
        return owner + 1 - 2 * lax.rem(owner, 2)

    upper = place >= blocks // 2

    def heads_of(owner):
        return jnp.where(upper, flipped(owner), owner)

    far = place + 2 * core - 1
    has_far = jnp.logical_and(far >= 0, far < blocks)
    crosses = jnp.logical_or(
        jnp.logical_and(place == blocks // 2 - 1, core == 1),
        jnp.logical_and(place == blocks // 2, core == 0),
    )
    sides = (
        (far, jnp.where(crosses, flipped(member), member)),
        (place + 1 - 2 * core, member),
    )

    def each_peer(body):
        lax.fori_loop(
            1, width, lambda _, code: (body(lax.rem(code, 8)), lax.div(code, 8))[1], jnp.int32(FAR_FIRST)
        )

    barrier = pltpu.get_barrier_semaphore()
    each_peer(
        lambda r: pl.semaphore_signal(
            barrier, inc=1, device_id=(place, peer(r)), device_id_type=MESH
        )
    )
    pl.semaphore_signal(barrier, inc=1, device_id=sides[CORE], device_id_type=MESH)

    spot, middle = lax.rem(place, blocks // 2), blocks // 4
    waits = jnp.logical_or(jnp.logical_and(core == 1, spot != middle - 1), spot == middle)
    greets_far = jnp.logical_and(has_far, jnp.logical_not(waits))
    waits_far = jnp.logical_and(has_far, waits)

    @pl.when(greets_far)
    def _():
        pl.semaphore_signal(barrier, inc=1, device_id=sides[FAR], device_id_type=MESH)

    pl.semaphore_wait(barrier, width + waits_far.astype(jnp.int32))

    @pl.when(waits_far)
    def _():
        pl.semaphore_signal(near, inc=1, device_id=sides[FAR], device_id_type=MESH)

    per_slot = block // CHUNK

    def piece(c):
        return slice(c * CHUNK, (c + 1) * CHUNK)

    def columns(owner, h):
        return pl.ds(pl.multiple_of((heads_of(owner) * 2 + h) * HEAD_DIM, HEAD_DIM), HEAD_DIM)

    def token_rows(owner):
        return pl.ds(pl.multiple_of(owner * rows, rows), rows)

    def landing(a, h):
        if a == Q:
            return q_buf.at[h]
        if a == G:
            return g_buf.at[h]
        return (k_buf if a == K else v_buf).at[h, OWN]

    def in_place(a, h):
        return landing(a, h).at[token_rows(member)]

    def wait_bytes(ref, sem):
        pltpu.make_async_copy(ref, ref, sem).wait()

    def in_copy(a, h, r):
        return pltpu.make_async_remote_copy(
            src_ref=inputs[a].at[:, columns(peer(r), h)],
            dst_ref=in_place(a, h),
            send_sem=in_send.at[a],
            recv_sem=in_recv.at[a, h],
            device_id=(place, peer(r)),
            device_id_type=MESH,
        )

    def in_own(a, h):
        return pltpu.make_async_copy(
            inputs[a].at[:, columns(member, h)], in_place(a, h), in_recv.at[a, h]
        )

    def send_in(a, h):
        each_peer(lambda r: in_copy(a, h, r).start())
        in_own(a, h).start()

    def wait_in(a, h):
        wait_bytes(landing(a, h), in_recv.at[a, h])

    def halo(a, h, side):
        buf, i = (k_buf, 0) if a == K else (v_buf, 1)
        return pltpu.make_async_remote_copy(
            src_ref=buf.at[h, OWN],
            dst_ref=buf.at[h, side],
            send_sem=halo_send.at[i, side],
            recv_sem=halo_recv.at[i, h, side],
            device_id=sides[side],
            device_id_type=MESH,
        )

    def edge(i, h, side, c):
        return pltpu.make_async_remote_copy(
            src_ref=edge_out.at[i, h, side, pl.ds(c * CHUNK, CHUNK)],
            dst_ref=edge_in.at[i, h, side, pl.ds(c * CHUNK, CHUNK)],
            send_sem=edge_send.at[i, side],
            recv_sem=edge_recv.at[i, h, side],
            device_id=sides[side],
            device_id_type=MESH,
        )

    def if_there(side, action):
        if side == FAR:
            pl.when(has_far)(action)
        else:
            action()

    def start_halo(a, h):
        for side in (FAR, CORE):
            if_there(side, halo(a, h, side).start)

    results = (o_buf, dq_buf, dk_buf, dv_buf)

    def out_copy(i, h, r):
        return pltpu.make_async_remote_copy(
            src_ref=results[i].at[h, token_rows(peer(r))],
            dst_ref=outputs[i].at[:, columns(member, h)],
            send_sem=out_send.at[i],
            recv_sem=out_recv.at[i],
            device_id=(place, peer(r)),
            device_id_type=MESH,
        )

    def out_own(i, h):
        return pltpu.make_async_copy(
            results[i].at[h, token_rows(member)],
            outputs[i].at[:, columns(member, h)],
            out_recv.at[i],
        )

    def send_out(i, h):
        each_peer(lambda r: out_copy(i, h, r).start())
        out_own(i, h).start()

    for a, h in ((K, 0), (V, 0), (Q, 0), (K, 1), (G, 0), (V, 1), (Q, 1), (G, 1)):
        send_in(a, h)

    @pl.when(jnp.logical_not(has_far))
    def _():
        k_buf[:, FAR] = jnp.zeros_like(k_buf[:, FAR])
        v_buf[:, FAR] = jnp.zeros_like(v_buf[:, FAR])
        edge_in[:, :, FAR] = jnp.zeros_like(edge_in[:, :, FAR])

    def slot_scores(h, slot, query_t):
        best = jnp.full((8, block), -jnp.inf, jnp.float32)
        for c in range(per_slot):
            part = dot(k_buf[h, slot, piece(c)], query_t)
            scores[slot, piece(c)] = part
            best = jnp.maximum(best, jnp.max(part.reshape(CHUNK // 8, 8, block), axis=0))
        if slot == FAR:
            best = jnp.where(has_far, best, -jnp.inf)
        return best

    def slot_weights(h, slot, top):
        if slot == FAR:
            top = jnp.where(has_far, top, jnp.float32(1e30))
        total = jnp.zeros((8, block), jnp.float32)
        acc = jnp.zeros((HEAD_DIM, block), jnp.float32)
        for c in range(per_slot):
            raised = jnp.exp2(scores[slot, piece(c)] * LOG2_SCALE - top)
            total = total + jnp.sum(raised.reshape(CHUNK // 8, 8, block), axis=0)
            low = raised.astype(jnp.bfloat16)
            weights[slot, piece(c)] = low
            acc = acc + dot(v_buf[h, slot, piece(c)].T, low)
        return total, acc

    def slot_grads(h, slot, query, grad, grad_t, row_dot, dk_ref, dv_ref):
        acc = jnp.zeros((HEAD_DIM, block), jnp.float32)
        for c in range(per_slot):
            low = weights[slot, piece(c)]
            grad_probs = dot(v_buf[h, slot, piece(c)], grad_t)
            grad_scores = (low.astype(jnp.float32) * (grad_probs - row_dot)).astype(jnp.bfloat16)
            dv_ref[piece(c)] = dot(low, grad).astype(dv_ref.dtype)
            dk_ref[piece(c)] = dot(grad_scores, query).astype(dk_ref.dtype)
            if slot != OWN:
                for i in range(2):
                    if_there(slot, edge(i, h, slot, c).start)
            acc = acc + dot(k_buf[h, slot, piece(c)].T, grad_scores)
        return acc

    def finish_keys(h):
        for i, (own, buf, scale) in enumerate(((own_dk, dk_buf, SCALE), (own_dv, dv_buf, 1.0))):
            for side in (CORE, FAR):
                if_there(
                    side, lambda: wait_bytes(edge_in.at[i, h, side], edge_recv.at[i, h, side])
                )
            total = (
                own[h]
                + edge_in[i, h, 0].astype(jnp.float32)
                + edge_in[i, h, 1].astype(jnp.float32)
            )
            buf[h] = (total * scale).astype(jnp.bfloat16)
            send_out(DK + i, h)

    def forward(a, h):
        wait_in(a, h)
        start_halo(a, h)

    def wait_halo(a, h, side):
        if_there(side, halo(a, h, side).wait_recv)

    @pl.when(greets_far)
    def _():
        pl.semaphore_wait(near, 1)

    forward(K, 0)
    forward(V, 0)
    for h in range(2):
        wait_in(Q, h)
        query = q_buf[h]
        query_t = query.T
        best = slot_scores(h, OWN, query_t)
        for slot in (CORE, FAR):
            wait_halo(K, h, slot)
            best = jnp.maximum(best, slot_scores(h, slot, query_t))
        top = jnp.max(best, axis=0, keepdims=True) * LOG2_SCALE
        total, acc = slot_weights(h, OWN, top)
        for slot in (CORE, FAR):
            if h == 0 and slot == FAR:
                forward(K, 1)
            wait_halo(V, h, slot)
            more, term = slot_weights(h, slot, top)
            total, acc = total + more, acc + term
        inverse = 1.0 / jnp.sum(total, axis=0, keepdims=True)
        attended_t = (acc * inverse).astype(jnp.bfloat16)
        o_buf[h] = attended_t.T
        send_out(O, h)
        wait_in(G, h)
        grad_t = (g_buf[h].T.astype(jnp.float32) * inverse).astype(jnp.bfloat16)
        row_dot = jnp.sum(
            grad_t.astype(jnp.float32) * attended_t.astype(jnp.float32), axis=0, keepdims=True
        )
        grad = grad_t.T
        acc = None
        for slot in (CORE, FAR) if h == 0 else (FAR, CORE):
            term = slot_grads(
                h, slot, query, grad, grad_t, row_dot, edge_out.at[0, h, slot], edge_out.at[1, h, slot]
            )
            if acc is None:
                acc = term
                if h == 0:
                    forward(V, 1)
                else:
                    finish_keys(0)
            else:
                acc = acc + term
        acc = acc + slot_grads(h, OWN, query, grad, grad_t, row_dot, own_dk.at[h], own_dv.at[h])
        dq_buf[h] = (acc * SCALE).astype(jnp.bfloat16).T
        send_out(DQ, h)
    others = pl.ds(0, (width - 1) * rows)
    for a, buf in ((Q, q_buf), (G, g_buf)):
        wait_bytes(buf.at[:, others], in_send.at[a])
    for i, buf in enumerate((k_buf, v_buf)):
        wait_bytes(buf.at[:, OWN, others], in_send.at[(K, V)[i]])
        for side in (FAR, CORE):
            if_there(side, lambda: wait_bytes(buf.at[:, side], halo_send.at[i, side]))
    finish_keys(1)

    for i in range(2):
        for side in (FAR, CORE):
            if_there(side, lambda: wait_bytes(edge_out.at[i, :, side], edge_send.at[i, side]))
    for i in range(4):
        wait_bytes(results[i].at[:, others], out_send.at[i])
        wait_bytes(outputs[i], out_recv.at[i])


def hand_over(*refs):
    sources, targets, done = refs[:4], refs[4:8], refs[8]
    count = done.shape[1]
    rows = sources[0].shape[0] // count
    copies = [
        pltpu.make_async_copy(
            sources[i].at[pl.ds(j * rows, rows)], targets[i].at[pl.ds(j * rows, rows)], done.at[i, j]
        )
        for i in range(4)
        for j in range(count)
    ]
    for copy in copies:
        copy.start()
    for copy in copies:
        copy.wait()


def local(query_in, key_in, value_in, out_grad):
    width = lax.axis_size("uly")
    rows, _ = query_in.shape
    block = rows * width
    heads = HEADS // width
    low, full = jnp.bfloat16, jnp.float32
    dma = pltpu.SemaphoreType.DMA
    whole = pl.BlockSpec(memory_space=pl.ANY)
    query_in, key_in, value_in, out_grad = (
        pltpu.with_memory_space_constraint(array, pltpu.HBM)
        for array in (query_in, key_in, value_in, out_grad)
    )
    results = pl.pallas_call(
        kernel,
        in_specs=[whole] * 4,
        out_specs=[whole] * 4,
        out_shape=[pltpu.VMEM(query_in.shape, low)] * 4,
        scratch_shapes=[
            pltpu.VMEM((heads, block, HEAD_DIM), low),
            pltpu.VMEM((heads, block, HEAD_DIM), low),
            pltpu.VMEM((heads, 3, block, HEAD_DIM), low),
            pltpu.VMEM((heads, 3, block, HEAD_DIM), low),
            pltpu.VMEM((3, block, block), full),
            pltpu.VMEM((3, block, block), low),
            pltpu.VMEM((heads, block, HEAD_DIM), low),
            pltpu.VMEM((heads, block, HEAD_DIM), low),
            pltpu.VMEM((heads, block, HEAD_DIM), low),
            pltpu.VMEM((heads, block, HEAD_DIM), low),
            pltpu.VMEM((heads, block, HEAD_DIM), full),
            pltpu.VMEM((heads, block, HEAD_DIM), full),
            pltpu.VMEM((2, heads, 2, block, HEAD_DIM), low),
            pltpu.VMEM((2, heads, 2, block, HEAD_DIM), low),
            dma((4,)),
            dma((4, heads)),
            dma((2, 2)),
            dma((2, heads, 2)),
            dma((2, 2)),
            dma((2, heads, 2)),
            dma((4,)),
            dma((4,)),
            pltpu.SemaphoreType.REGULAR,
        ],
        compiler_params=pltpu.CompilerParams(
            collective_id=0, has_side_effects=True, vmem_limit_bytes=44 * 2**20
        ),
        cost_estimate=pl.CostEstimate(
            flops=12 * heads * 3 * block * block * HEAD_DIM,
            bytes_accessed=16 * rows * HEADS * HEAD_DIM,
            transcendentals=heads * 3 * block * block,
        ),
    )(query_in, key_in, value_in, out_grad)
    return pl.pallas_call(
        hand_over,
        in_specs=[whole] * 4,
        out_specs=[whole] * 4,
        out_shape=[jax.ShapeDtypeStruct(query_in.shape, low)] * 4,
        scratch_shapes=[dma((4, 1))],
    )(*(pltpu.with_memory_space_constraint(result, pltpu.VMEM) for result in results))


def solution(mesh):
    spec = P(("blk", "uly"), None)
    return jax.shard_map(
        local,
        mesh=mesh,
        in_specs=(spec,) * 4,
        out_specs=(spec,) * 4,
        check_vma=False,
    )
```

```python
import jax
import jax.numpy as jnp
from jax import lax
from jax.experimental import pallas as pl
from jax.experimental.pallas import tpu as pltpu
from jax.sharding import PartitionSpec as P

HEADS = 16
HEAD_DIM = 128
SCALE = HEAD_DIM ** (-0.5)
LOG2_SCALE = SCALE * 1.4426950408889634
MESH = pl.DeviceIdType.MESH
CHUNK = 512
Q, K, V, G = range(4)
O, DQ, DK, DV = range(4)
FAR, CORE, OWN = range(3)
FAR_FIRST = 0o6214735


def dot(a, b):
    return jnp.dot(a, b, preferred_element_type=jnp.float32)


def kernel(
    q_in, k_in, v_in, g_in, o_out, dq_out, dk_out, dv_out,
    q_buf, g_buf, k_buf, v_buf, scores, weights, o_buf, dq_buf, dk_buf, dv_buf,
    own_dk, own_dv, edge_out, edge_in,
    in_send, in_recv, first_recv, halo_send, halo_recv, edge_send, edge_recv, out_send, out_recv, near,
):
    rows = q_in.shape[0]
    block = q_buf.shape[1]
    blocks = lax.axis_size("blk")
    width = lax.axis_size("uly")
    place = lax.axis_index("blk")
    member = lax.axis_index("uly")
    core = lax.rem(place, 2)
    column_x, column_y = lax.div(member, 2), lax.rem(member, 2)
    inputs, outputs = (q_in, k_in, v_in, g_in), (o_out, dq_out, dk_out, dv_out)

    def peer(r):
        x = lax.rem(column_x + lax.div(r, 2), width // 2)
        y = lax.rem(column_y + lax.rem(r, 2), 2)
        return x * 2 + y

    def source(r):
        x = lax.rem(column_x + width // 2 - lax.div(r, 2), width // 2)
        y = lax.rem(column_y + lax.rem(r, 2), 2)
        return x * 2 + y

    def flipped(owner):
        return owner + 1 - 2 * lax.rem(owner, 2)

    upper = place >= blocks // 2

    def heads_of(owner):
        return jnp.where(upper, flipped(owner), owner)

    far = place + 2 * core - 1
    has_far = jnp.logical_and(far >= 0, far < blocks)
    crosses = jnp.logical_or(
        jnp.logical_and(place == blocks // 2 - 1, core == 1),
        jnp.logical_and(place == blocks // 2, core == 0),
    )
    sides = (
        (far, jnp.where(crosses, flipped(member), member)),
        (place + 1 - 2 * core, member),
    )

    def each_peer(body):
        lax.fori_loop(
            1, width, lambda _, code: (body(lax.rem(code, 8)), lax.div(code, 8))[1], jnp.int32(FAR_FIRST)
        )

    spot, middle = lax.rem(place, blocks // 2), blocks // 4
    waits = jnp.logical_or(jnp.logical_and(core == 1, spot != middle - 1), spot == middle)
    greets_far = jnp.logical_and(has_far, jnp.logical_not(waits))
    waits_far = jnp.logical_and(has_far, waits)

    barrier = pltpu.get_barrier_semaphore()

    @pl.when(greets_far)
    def _():
        pl.semaphore_signal(barrier, inc=1, device_id=sides[FAR], device_id_type=MESH)

    each_peer(
        lambda r: pl.semaphore_signal(
            barrier, inc=1, device_id=(place, peer(r)), device_id_type=MESH
        )
    )
    pl.semaphore_signal(barrier, inc=1, device_id=sides[CORE], device_id_type=MESH)

    per_slot = block // CHUNK

    def piece(c):
        return slice(c * CHUNK, (c + 1) * CHUNK)

    def columns(owner, h):
        return pl.ds(pl.multiple_of((heads_of(owner) * 2 + h) * HEAD_DIM, HEAD_DIM), HEAD_DIM)

    def token_rows(owner):
        return pl.ds(pl.multiple_of(owner * rows, rows), rows)

    def landing(a, h):
        if a == Q:
            return q_buf.at[h]
        if a == G:
            return g_buf.at[h]
        return (k_buf if a == K else v_buf).at[h, OWN]

    def arrived(a, h, r):
        return first_recv.at[(K, V).index(a), r] if h == 0 and a in (K, V) else in_recv.at[a, h]

    def in_place(a, h):
        return landing(a, h).at[token_rows(member)]

    def wait_bytes(ref, sem):
        pltpu.make_async_copy(ref, ref, sem).wait()

    def in_copy(a, h, r):
        return pltpu.make_async_remote_copy(
            src_ref=inputs[a].at[:, columns(peer(r), h)],
            dst_ref=in_place(a, h),
            send_sem=in_send.at[a],
            recv_sem=arrived(a, h, r),
            device_id=(place, peer(r)),
            device_id_type=MESH,
        )

    def in_own(a, h):
        return pltpu.make_async_copy(
            inputs[a].at[:, columns(member, h)], in_place(a, h), arrived(a, h, 0)
        )

    def send_in(a, h):
        each_peer(lambda r: in_copy(a, h, r).start())

    def wait_in(a, h):
        wait_bytes(landing(a, h), in_recv.at[a, h])

    def halo(a, h, side, part=slice(None)):
        buf, i = (k_buf, 0) if a == K else (v_buf, 1)
        return pltpu.make_async_remote_copy(
            src_ref=buf.at[h, OWN, part],
            dst_ref=buf.at[h, side, part],
            send_sem=halo_send.at[i, side],
            recv_sem=halo_recv.at[i, h, side],
            device_id=sides[side],
            device_id_type=MESH,
        )

    def edge(i, h, side, c):
        return pltpu.make_async_remote_copy(
            src_ref=edge_out.at[i, h, side, pl.ds(c * CHUNK, CHUNK)],
            dst_ref=edge_in.at[i, h, side, pl.ds(c * CHUNK, CHUNK)],
            send_sem=edge_send.at[i, side],
            recv_sem=edge_recv.at[i, h, side],
            device_id=sides[side],
            device_id_type=MESH,
        )

    def if_there(side, action):
        if side == FAR:
            pl.when(has_far)(action)
        else:
            action()

    def start_halo(a, h):
        for side in (FAR, CORE):
            if_there(side, halo(a, h, side).start)

    results = (o_buf, dq_buf, dk_buf, dv_buf)

    def out_copy(i, h, r):
        return pltpu.make_async_remote_copy(
            src_ref=results[i].at[h, token_rows(peer(r))],
            dst_ref=outputs[i].at[:, columns(member, h)],
            send_sem=out_send.at[i],
            recv_sem=out_recv.at[i],
            device_id=(place, peer(r)),
            device_id_type=MESH,
        )

    def out_own(i, h):
        return pltpu.make_async_copy(
            results[i].at[h, token_rows(member)],
            outputs[i].at[:, columns(member, h)],
            out_recv.at[i],
        )

    def send_out(i, h):
        each_peer(lambda r: out_copy(i, h, r).start())
        out_own(i, h).start()

    order = ((K, 0), (V, 0), (Q, 0), (K, 1), (G, 0), (V, 1), (Q, 1), (G, 1))
    for a, h in order:
        in_own(a, h).start()

    pl.semaphore_wait(barrier, width + waits_far.astype(jnp.int32))

    @pl.when(waits_far)
    def _():
        pl.semaphore_signal(near, inc=1, device_id=sides[FAR], device_id_type=MESH)

    for a, h in order:
        send_in(a, h)

    @pl.when(jnp.logical_not(has_far))
    def _():
        k_buf[:, FAR] = jnp.zeros_like(k_buf[:, FAR])
        v_buf[:, FAR] = jnp.zeros_like(v_buf[:, FAR])
        edge_in[:, :, FAR] = jnp.zeros_like(edge_in[:, :, FAR])

    def slot_scores(h, slot, query_t):
        best = jnp.full((8, block), -jnp.inf, jnp.float32)
        for c in range(per_slot):
            part = dot(k_buf[h, slot, piece(c)], query_t)
            scores[slot, piece(c)] = part
            best = jnp.maximum(best, jnp.max(part.reshape(CHUNK // 8, 8, block), axis=0))
        if slot == FAR:
            best = jnp.where(has_far, best, -jnp.inf)
        return best

    def slot_weights(h, slot, top):
        if slot == FAR:
            top = jnp.where(has_far, top, jnp.float32(1e30))
        total = jnp.zeros((8, block), jnp.float32)
        acc = jnp.zeros((HEAD_DIM, block), jnp.float32)
        for c in range(per_slot):
            raised = jnp.exp2(scores[slot, piece(c)] * LOG2_SCALE - top)
            total = total + jnp.sum(raised.reshape(CHUNK // 8, 8, block), axis=0)
            low = raised.astype(jnp.bfloat16)
            weights[slot, piece(c)] = low
            acc = acc + dot(v_buf[h, slot, piece(c)].T, low)
        return total, acc

    def slot_grads(h, slot, query, grad, grad_t, row_dot, dk_ref, dv_ref):
        acc = jnp.zeros((HEAD_DIM, block), jnp.float32)
        for c in range(per_slot):
            low = weights[slot, piece(c)]
            grad_probs = dot(v_buf[h, slot, piece(c)], grad_t)
            grad_scores = (low.astype(jnp.float32) * (grad_probs - row_dot)).astype(jnp.bfloat16)
            dv_ref[piece(c)] = dot(low, grad).astype(dv_ref.dtype)
            dk_ref[piece(c)] = dot(grad_scores, query).astype(dk_ref.dtype)
            if slot != OWN:
                for i in range(2):
                    if_there(slot, edge(i, h, slot, c).start)
            acc = acc + dot(k_buf[h, slot, piece(c)].T, grad_scores)
        return acc

    def finish_keys(h):
        for i, (own, buf, scale) in enumerate(((own_dk, dk_buf, SCALE), (own_dv, dv_buf, 1.0))):
            for side in (CORE, FAR):
                if_there(
                    side, lambda: wait_bytes(edge_in.at[i, h, side], edge_recv.at[i, h, side])
                )
            total = (
                own[h]
                + edge_in[i, h, 0].astype(jnp.float32)
                + edge_in[i, h, 1].astype(jnp.float32)
            )
            buf[h] = (total * scale).astype(jnp.bfloat16)
            send_out(DK + i, h)

    def forward(a, h):
        wait_in(a, h)
        start_halo(a, h)

    def forward_pieces(a):
        def step(r):
            part = token_rows(source(r))
            wait_bytes(landing(a, 0).at[part], arrived(a, 0, r))
            for side in (FAR, CORE):
                if_there(side, halo(a, 0, side, part).start)

        step(jnp.int32(0))
        each_peer(step)

    def wait_halo(a, h, side):
        if_there(side, halo(a, h, side).wait_recv)

    @pl.when(greets_far)
    def _():
        pl.semaphore_wait(near, 1)

    forward_pieces(K)
    forward_pieces(V)
    for h in range(2):
        wait_in(Q, h)
        query = q_buf[h]
        query_t = query.T
        best = slot_scores(h, OWN, query_t)
        for slot in (CORE, FAR):
            wait_halo(K, h, slot)
            best = jnp.maximum(best, slot_scores(h, slot, query_t))
        top = jnp.max(best, axis=0, keepdims=True) * LOG2_SCALE
        total, acc = slot_weights(h, OWN, top)
        for slot in (CORE, FAR):
            if h == 0 and slot == FAR:
                forward(K, 1)
            wait_halo(V, h, slot)
            more, term = slot_weights(h, slot, top)
            total, acc = total + more, acc + term
        inverse = 1.0 / jnp.sum(total, axis=0, keepdims=True)
        attended_t = (acc * inverse).astype(jnp.bfloat16)
        o_buf[h] = attended_t.T
        send_out(O, h)
        wait_in(G, h)
        grad_t = (g_buf[h].T.astype(jnp.float32) * inverse).astype(jnp.bfloat16)
        row_dot = jnp.sum(
            grad_t.astype(jnp.float32) * attended_t.astype(jnp.float32), axis=0, keepdims=True
        )
        grad = grad_t.T
        acc = None
        for slot in (CORE, FAR) if h == 0 else (FAR, CORE):
            term = slot_grads(
                h, slot, query, grad, grad_t, row_dot, edge_out.at[0, h, slot], edge_out.at[1, h, slot]
            )
            if acc is None:
                acc = term
                if h == 0:
                    forward(V, 1)
                else:
                    finish_keys(0)
            else:
                acc = acc + term
        acc = acc + slot_grads(h, OWN, query, grad, grad_t, row_dot, own_dk.at[h], own_dv.at[h])
        dq_buf[h] = (acc * SCALE).astype(jnp.bfloat16).T
        send_out(DQ, h)
    others = pl.ds(0, (width - 1) * rows)
    for a, buf in ((Q, q_buf), (G, g_buf)):
        wait_bytes(buf.at[:, others], in_send.at[a])
    for i, buf in enumerate((k_buf, v_buf)):
        wait_bytes(buf.at[:, OWN, others], in_send.at[(K, V)[i]])
        for side in (FAR, CORE):
            if_there(side, lambda: wait_bytes(buf.at[:, side], halo_send.at[i, side]))
    finish_keys(1)

    for i in range(2):
        for side in (FAR, CORE):
            if_there(side, lambda: wait_bytes(edge_out.at[i, :, side], edge_send.at[i, side]))
    for i in range(4):
        wait_bytes(results[i].at[:, others], out_send.at[i])
        wait_bytes(outputs[i], out_recv.at[i])


def hand_over(*refs):
    sources, targets, done = refs[:4], refs[4:8], refs[8]
    count = done.shape[1]
    rows = sources[0].shape[0] // count
    copies = [
        pltpu.make_async_copy(
            sources[i].at[pl.ds(j * rows, rows)], targets[i].at[pl.ds(j * rows, rows)], done.at[i, j]
        )
        for i in range(4)
        for j in range(count)
    ]
    for copy in copies:
        copy.start()
    for copy in copies:
        copy.wait()


def local(query_in, key_in, value_in, out_grad):
    width = lax.axis_size("uly")
    rows, _ = query_in.shape
    block = rows * width
    heads = HEADS // width
    low, full = jnp.bfloat16, jnp.float32
    dma = pltpu.SemaphoreType.DMA
    whole = pl.BlockSpec(memory_space=pl.ANY)
    query_in, key_in, value_in, out_grad = (
        pltpu.with_memory_space_constraint(array, pltpu.HBM)
        for array in (query_in, key_in, value_in, out_grad)
    )
    results = pl.pallas_call(
        kernel,
        in_specs=[whole] * 4,
        out_specs=[whole] * 4,
        out_shape=[pltpu.VMEM(query_in.shape, low)] * 4,
        scratch_shapes=[
            pltpu.VMEM((heads, block, HEAD_DIM), low),
            pltpu.VMEM((heads, block, HEAD_DIM), low),
            pltpu.VMEM((heads, 3, block, HEAD_DIM), low),
            pltpu.VMEM((heads, 3, block, HEAD_DIM), low),
            pltpu.VMEM((3, block, block), full),
            pltpu.VMEM((3, block, block), low),
            pltpu.VMEM((heads, block, HEAD_DIM), low),
            pltpu.VMEM((heads, block, HEAD_DIM), low),
            pltpu.VMEM((heads, block, HEAD_DIM), low),
            pltpu.VMEM((heads, block, HEAD_DIM), low),
            pltpu.VMEM((heads, block, HEAD_DIM), full),
            pltpu.VMEM((heads, block, HEAD_DIM), full),
            pltpu.VMEM((2, heads, 2, block, HEAD_DIM), low),
            pltpu.VMEM((2, heads, 2, block, HEAD_DIM), low),
            dma((4,)),
            dma((4, heads)),
            dma((2, width)),
            dma((2, 2)),
            dma((2, heads, 2)),
            dma((2, 2)),
            dma((2, heads, 2)),
            dma((4,)),
            dma((4,)),
            pltpu.SemaphoreType.REGULAR,
        ],
        compiler_params=pltpu.CompilerParams(
            collective_id=0, has_side_effects=True, vmem_limit_bytes=44 * 2**20
        ),
        cost_estimate=pl.CostEstimate(
            flops=12 * heads * 3 * block * block * HEAD_DIM,
            bytes_accessed=16 * rows * HEADS * HEAD_DIM,
            transcendentals=heads * 3 * block * block,
        ),
    )(query_in, key_in, value_in, out_grad)
    return pl.pallas_call(
        hand_over,
        in_specs=[whole] * 4,
        out_specs=[whole] * 4,
        out_shape=[jax.ShapeDtypeStruct(query_in.shape, low)] * 4,
        scratch_shapes=[dma((4, 1))],
    )(*(pltpu.with_memory_space_constraint(result, pltpu.VMEM) for result in results))


def solution(mesh):
    spec = P(("blk", "uly"), None)
    return jax.shard_map(
        local,
        mesh=mesh,
        in_specs=(spec,) * 4,
        out_specs=(spec,) * 4,
        check_vma=False,
    )
```

```python
import jax
import jax.numpy as jnp
from jax import lax
from jax.experimental import pallas as pl
from jax.experimental.pallas import tpu as pltpu
from jax.sharding import PartitionSpec as P

HEADS = 16
HEAD_DIM = 128
SCALE = HEAD_DIM ** (-0.5)
LOG2_SCALE = SCALE * 1.4426950408889634
MESH = pl.DeviceIdType.MESH
CHUNK = 512
Q, K, V, G = range(4)
O, DQ, DK, DV = range(4)
FAR, CORE, OWN = range(3)
FAR_FIRST = 0o6214735


def dot(a, b):
    return jnp.dot(a, b, preferred_element_type=jnp.float32)


def kernel(
    q_in, k_in, v_in, g_in, o_out, dq_out, dk_out, dv_out,
    q_buf, g_buf, k_buf, v_buf, scores, weights, o_buf, dq_buf, dk_buf, dv_buf,
    own_dk, own_dv, edge_out, edge_in,
    in_send, in_recv, first_recv, halo_send, halo_recv, edge_send, edge_recv, out_send, out_recv, near,
):
    rows = q_in.shape[0]
    block = q_buf.shape[1]
    blocks = lax.axis_size("blk")
    width = lax.axis_size("uly")
    place = lax.axis_index("blk")
    member = lax.axis_index("uly")
    core = lax.rem(place, 2)
    column_x, column_y = lax.div(member, 2), lax.rem(member, 2)
    inputs, outputs = (q_in, k_in, v_in, g_in), (o_out, dq_out, dk_out, dv_out)

    def peer(r):
        x = lax.rem(column_x + lax.div(r, 2), width // 2)
        y = lax.rem(column_y + lax.rem(r, 2), 2)
        return x * 2 + y

    def source(r):
        x = lax.rem(column_x + width // 2 - lax.div(r, 2), width // 2)
        y = lax.rem(column_y + lax.rem(r, 2), 2)
        return x * 2 + y

    def flipped(owner):
        return owner + 1 - 2 * lax.rem(owner, 2)

    upper = place >= blocks // 2

    def heads_of(owner):
        return jnp.where(upper, flipped(owner), owner)

    far = place + 2 * core - 1
    has_far = jnp.logical_and(far >= 0, far < blocks)
    crosses = jnp.logical_or(
        jnp.logical_and(place == blocks // 2 - 1, core == 1),
        jnp.logical_and(place == blocks // 2, core == 0),
    )
    sides = (
        (far, jnp.where(crosses, flipped(member), member)),
        (place + 1 - 2 * core, member),
    )

    def each_peer(body):
        lax.fori_loop(
            1, width, lambda _, code: (body(lax.rem(code, 8)), lax.div(code, 8))[1], jnp.int32(FAR_FIRST)
        )

    spot, middle = lax.rem(place, blocks // 2), blocks // 4
    waits = jnp.logical_or(jnp.logical_and(core == 1, spot != middle - 1), spot == middle)
    greets_far = jnp.logical_and(has_far, jnp.logical_not(waits))
    waits_far = jnp.logical_and(has_far, waits)

    barrier = pltpu.get_barrier_semaphore()

    @pl.when(greets_far)
    def _():
        pl.semaphore_signal(barrier, inc=1, device_id=sides[FAR], device_id_type=MESH)

    each_peer(
        lambda r: pl.semaphore_signal(
            barrier, inc=1, device_id=(place, peer(r)), device_id_type=MESH
        )
    )
    pl.semaphore_signal(barrier, inc=1, device_id=sides[CORE], device_id_type=MESH)

    per_slot = block // CHUNK

    def piece(c):
        return slice(c * CHUNK, (c + 1) * CHUNK)

    def columns(owner, h):
        return pl.ds(pl.multiple_of((heads_of(owner) * 2 + h) * HEAD_DIM, HEAD_DIM), HEAD_DIM)

    def token_rows(owner):
        return pl.ds(pl.multiple_of(owner * rows, rows), rows)

    def landing(a, h):
        if a == Q:
            return q_buf.at[h]
        if a == G:
            return g_buf.at[h]
        return (k_buf if a == K else v_buf).at[h, OWN]

    def arrived(a, h, r):
        return first_recv.at[(K, V).index(a), r] if h == 0 and a in (K, V) else in_recv.at[a, h]

    def in_place(a, h):
        return landing(a, h).at[token_rows(member)]

    def wait_bytes(ref, sem):
        pltpu.make_async_copy(ref, ref, sem).wait()

    def in_copy(a, h, r):
        return pltpu.make_async_remote_copy(
            src_ref=inputs[a].at[:, columns(peer(r), h)],
            dst_ref=in_place(a, h),
            send_sem=in_send.at[0],
            recv_sem=arrived(a, h, r),
            device_id=(place, peer(r)),
            device_id_type=MESH,
        )

    def in_own(a, h):
        return pltpu.make_async_copy(
            inputs[a].at[:, columns(member, h)], in_place(a, h), arrived(a, h, 0)
        )

    def send_in(a, h):
        each_peer(lambda r: in_copy(a, h, r).start())

    def wait_in(a, h):
        wait_bytes(landing(a, h), in_recv.at[a, h])

    def halo(a, h, side, part=slice(None)):
        buf, i = (k_buf, 0) if a == K else (v_buf, 1)
        return pltpu.make_async_remote_copy(
            src_ref=buf.at[h, OWN, part],
            dst_ref=buf.at[h, side, part],
            send_sem=halo_send.at[side],
            recv_sem=halo_recv.at[i, h, side],
            device_id=sides[side],
            device_id_type=MESH,
        )

    def edge(i, h, side):
        return pltpu.make_async_remote_copy(
            src_ref=edge_out.at[i, h, side],
            dst_ref=edge_in.at[i, h, side],
            send_sem=edge_send.at[side],
            recv_sem=edge_recv.at[i, h, side],
            device_id=sides[side],
            device_id_type=MESH,
        )

    def if_there(side, action):
        if side == FAR:
            pl.when(has_far)(action)
        else:
            action()

    def start_halo(a, h):
        for side in (FAR, CORE):
            if_there(side, halo(a, h, side).start)

    results = (o_buf, dq_buf, dk_buf, dv_buf)

    def out_copy(i, h, r):
        return pltpu.make_async_remote_copy(
            src_ref=results[i].at[h, token_rows(peer(r))],
            dst_ref=outputs[i].at[:, columns(member, h)],
            send_sem=out_send.at[0],
            recv_sem=out_recv.at[i],
            device_id=(place, peer(r)),
            device_id_type=MESH,
        )

    def out_own(i, h):
        return pltpu.make_async_copy(
            results[i].at[h, token_rows(member)],
            outputs[i].at[:, columns(member, h)],
            out_recv.at[i],
        )

    def send_out(i, h):
        each_peer(lambda r: out_copy(i, h, r).start())
        out_own(i, h).start()

    order = ((K, 0), (V, 0), (Q, 0), (K, 1), (G, 0), (V, 1), (Q, 1), (G, 1))
    for a, h in order:
        in_own(a, h).start()

    pl.semaphore_wait(barrier, width + waits_far.astype(jnp.int32))

    @pl.when(waits_far)
    def _():
        pl.semaphore_signal(near, inc=1, device_id=sides[FAR], device_id_type=MESH)

    for a, h in order:
        send_in(a, h)

    @pl.when(jnp.logical_not(has_far))
    def _():
        k_buf[:, FAR] = jnp.zeros_like(k_buf[:, FAR])
        v_buf[:, FAR] = jnp.zeros_like(v_buf[:, FAR])
        edge_in[:, :, FAR] = jnp.zeros_like(edge_in[:, :, FAR])

    def slot_scores(h, slot, query_t):
        best = jnp.full((8, block), -jnp.inf, jnp.float32)
        for c in range(per_slot):
            part = dot(k_buf[h, slot, piece(c)], query_t)
            scores[slot, piece(c)] = part
            best = jnp.maximum(best, jnp.max(part.reshape(CHUNK // 8, 8, block), axis=0))
        if slot == FAR:
            best = jnp.where(has_far, best, -jnp.inf)
        return best

    def slot_weights(h, slot, top):
        if slot == FAR:
            top = jnp.where(has_far, top, jnp.float32(1e30))
        total = jnp.zeros((8, block), jnp.float32)
        acc = jnp.zeros((HEAD_DIM, block), jnp.float32)
        for c in range(per_slot):
            raised = jnp.exp2(scores[slot, piece(c)] * LOG2_SCALE - top)
            total = total + jnp.sum(raised.reshape(CHUNK // 8, 8, block), axis=0)
            low = raised.astype(jnp.bfloat16)
            weights[slot, piece(c)] = low
            acc = acc + dot(v_buf[h, slot, piece(c)].T, low)
        return total, acc

    def slot_grads(h, slot, query, grad, grad_t, row_dot, dk_ref, dv_ref):
        acc = jnp.zeros((HEAD_DIM, block), jnp.float32)
        for c in range(per_slot):
            low = weights[slot, piece(c)]
            grad_probs = dot(v_buf[h, slot, piece(c)], grad_t)
            grad_scores = (low.astype(jnp.float32) * (grad_probs - row_dot)).astype(jnp.bfloat16)
            dv_ref[piece(c)] = dot(low, grad).astype(dv_ref.dtype)
            dk_ref[piece(c)] = dot(grad_scores, query).astype(dk_ref.dtype)
            acc = acc + dot(k_buf[h, slot, piece(c)].T, grad_scores)
        if slot != OWN:
            for i in range(2):
                if_there(slot, edge(i, h, slot).start)
        return acc

    def finish_keys(h):
        for i, (own, buf, scale) in enumerate(((own_dk, dk_buf, SCALE), (own_dv, dv_buf, 1.0))):
            for side in (CORE, FAR):
                if_there(
                    side, lambda: wait_bytes(edge_in.at[i, h, side], edge_recv.at[i, h, side])
                )
            total = (
                own[h]
                + edge_in[i, h, 0].astype(jnp.float32)
                + edge_in[i, h, 1].astype(jnp.float32)
            )
            buf[h] = (total * scale).astype(jnp.bfloat16)
            send_out(DK + i, h)

    def forward(a, h):
        wait_in(a, h)
        start_halo(a, h)

    def forward_pieces(a):
        def step(r):
            part = token_rows(source(r))
            wait_bytes(landing(a, 0).at[part], arrived(a, 0, r))
            for side in (FAR, CORE):
                if_there(side, halo(a, 0, side, part).start)

        step(jnp.int32(0))
        each_peer(step)

    def wait_halo(a, h, side):
        if_there(side, halo(a, h, side).wait_recv)

    @pl.when(greets_far)
    def _():
        pl.semaphore_wait(near, 1)

    forward_pieces(K)
    forward_pieces(V)
    for h in range(2):
        wait_in(Q, h)
        query = q_buf[h]
        query_t = query.T
        best = slot_scores(h, OWN, query_t)
        for slot in (CORE, FAR):
            wait_halo(K, h, slot)
            best = jnp.maximum(best, slot_scores(h, slot, query_t))
        top = jnp.max(best, axis=0, keepdims=True) * LOG2_SCALE
        total, acc = slot_weights(h, OWN, top)
        for slot in (CORE, FAR):
            if h == 0 and slot == FAR:
                forward(K, 1)
            wait_halo(V, h, slot)
            more, term = slot_weights(h, slot, top)
            total, acc = total + more, acc + term
        inverse = 1.0 / jnp.sum(total, axis=0, keepdims=True)
        attended_t = (acc * inverse).astype(jnp.bfloat16)
        o_buf[h] = attended_t.T
        send_out(O, h)
        wait_in(G, h)
        grad_t = (g_buf[h].T.astype(jnp.float32) * inverse).astype(jnp.bfloat16)
        row_dot = jnp.sum(
            grad_t.astype(jnp.float32) * attended_t.astype(jnp.float32), axis=0, keepdims=True
        )
        grad = grad_t.T
        acc = None
        for slot in (CORE, FAR) if h == 0 else (FAR, CORE):
            term = slot_grads(
                h, slot, query, grad, grad_t, row_dot, edge_out.at[0, h, slot], edge_out.at[1, h, slot]
            )
            if acc is None:
                acc = term
                if h == 0:
                    forward(V, 1)
                else:
                    finish_keys(0)
            else:
                acc = acc + term
        acc = acc + slot_grads(h, OWN, query, grad, grad_t, row_dot, own_dk.at[h], own_dv.at[h])
        dq_buf[h] = (acc * SCALE).astype(jnp.bfloat16).T
        send_out(DQ, h)
    one_side, to_others = edge_out.at[:, :, 0], edge_out.at[:, :, :, pl.ds(0, (width - 1) * rows)]
    wait_bytes(to_others, in_send.at[0])
    for side in (FAR, CORE):
        if_there(side, lambda: wait_bytes(one_side, halo_send.at[side]))
    finish_keys(1)

    for side in (FAR, CORE):
        if_there(side, lambda: wait_bytes(one_side, edge_send.at[side]))
    wait_bytes(to_others, out_send.at[0])
    for i in range(4):
        wait_bytes(outputs[i], out_recv.at[i])


def hand_over(*refs):
    sources, targets, done = refs[:4], refs[4:8], refs[8]
    count = done.shape[1]
    rows = sources[0].shape[0] // count
    copies = [
        pltpu.make_async_copy(
            sources[i].at[pl.ds(j * rows, rows)], targets[i].at[pl.ds(j * rows, rows)], done.at[i, j]
        )
        for i in range(4)
        for j in range(count)
    ]
    for copy in copies:
        copy.start()
    for copy in copies:
        copy.wait()


def local(query_in, key_in, value_in, out_grad):
    width = lax.axis_size("uly")
    rows, _ = query_in.shape
    block = rows * width
    heads = HEADS // width
    low, full = jnp.bfloat16, jnp.float32
    dma = pltpu.SemaphoreType.DMA
    whole = pl.BlockSpec(memory_space=pl.ANY)
    query_in, key_in, value_in, out_grad = (
        pltpu.with_memory_space_constraint(array, pltpu.HBM)
        for array in (query_in, key_in, value_in, out_grad)
    )
    results = pl.pallas_call(
        kernel,
        in_specs=[whole] * 4,
        out_specs=[whole] * 4,
        out_shape=[pltpu.VMEM(query_in.shape, low)] * 4,
        scratch_shapes=[
            pltpu.VMEM((heads, block, HEAD_DIM), low),
            pltpu.VMEM((heads, block, HEAD_DIM), low),
            pltpu.VMEM((heads, 3, block, HEAD_DIM), low),
            pltpu.VMEM((heads, 3, block, HEAD_DIM), low),
            pltpu.VMEM((3, block, block), full),
            pltpu.VMEM((3, block, block), low),
            pltpu.VMEM((heads, block, HEAD_DIM), low),
            pltpu.VMEM((heads, block, HEAD_DIM), low),
            pltpu.VMEM((heads, block, HEAD_DIM), low),
            pltpu.VMEM((heads, block, HEAD_DIM), low),
            pltpu.VMEM((heads, block, HEAD_DIM), full),
            pltpu.VMEM((heads, block, HEAD_DIM), full),
            pltpu.VMEM((2, heads, 2, block, HEAD_DIM), low),
            pltpu.VMEM((2, heads, 2, block, HEAD_DIM), low),
            dma((1,)),
            dma((4, heads)),
            dma((2, width)),
            dma((2,)),
            dma((2, heads, 2)),
            dma((2,)),
            dma((2, heads, 2)),
            dma((1,)),
            dma((4,)),
            pltpu.SemaphoreType.REGULAR,
        ],
        compiler_params=pltpu.CompilerParams(
            collective_id=0, has_side_effects=True, vmem_limit_bytes=44 * 2**20
        ),
        cost_estimate=pl.CostEstimate(
            flops=12 * heads * 3 * block * block * HEAD_DIM,
            bytes_accessed=16 * rows * HEADS * HEAD_DIM,
            transcendentals=heads * 3 * block * block,
        ),
    )(query_in, key_in, value_in, out_grad)
    return pl.pallas_call(
        hand_over,
        in_specs=[whole] * 4,
        out_specs=[whole] * 4,
        out_shape=[jax.ShapeDtypeStruct(query_in.shape, low)] * 4,
        scratch_shapes=[dma((4, 1))],
    )(*(pltpu.with_memory_space_constraint(result, pltpu.VMEM) for result in results))


def solution(mesh):
    spec = P(("blk", "uly"), None)
    return jax.shard_map(
        local,
        mesh=mesh,
        in_specs=(spec,) * 4,
        out_specs=(spec,) * 4,
        check_vma=False,
    )
```

```python
import jax
import jax.numpy as jnp
from jax import lax
from jax.experimental import pallas as pl
from jax.experimental.pallas import tpu as pltpu
from jax.sharding import PartitionSpec as P

HEADS = 16
HEAD_DIM = 128
SCALE = HEAD_DIM ** (-0.5)
LOG2_SCALE = SCALE * 1.4426950408889634
MESH = pl.DeviceIdType.MESH
CHUNK = 512
SCORE_CHUNK = 256
Q, K, V, G = range(4)
O, DQ, DK, DV = range(4)
FAR, CORE, OWN = range(3)
FAR_FIRST = 0o6214735


def dot(a, b):
    return jnp.dot(a, b, preferred_element_type=jnp.float32)


def kernel(
    q_in, k_in, v_in, g_in, o_out, dq_out, dk_out, dv_out,
    q_buf, g_buf, k_buf, v_buf, scores, weights, o_buf, dq_buf, dk_buf, dv_buf,
    own_dk, own_dv, edge_out, edge_in,
    in_send, in_recv, first_recv, halo_send, halo_recv, edge_send, edge_recv, out_send, out_recv, near,
):
    rows = q_in.shape[0]
    block = q_buf.shape[1]
    blocks = lax.axis_size("blk")
    width = lax.axis_size("uly")
    place = lax.axis_index("blk")
    member = lax.axis_index("uly")
    core = lax.rem(place, 2)
    column_x, column_y = lax.div(member, 2), lax.rem(member, 2)
    inputs, outputs = (q_in, k_in, v_in, g_in), (o_out, dq_out, dk_out, dv_out)

    def peer(r):
        x = lax.rem(column_x + lax.div(r, 2), width // 2)
        y = lax.rem(column_y + lax.rem(r, 2), 2)
        return x * 2 + y

    def source(r):
        x = lax.rem(column_x + width // 2 - lax.div(r, 2), width // 2)
        y = lax.rem(column_y + lax.rem(r, 2), 2)
        return x * 2 + y

    def flipped(owner):
        return owner + 1 - 2 * lax.rem(owner, 2)

    upper = place >= blocks // 2

    def heads_of(owner):
        return jnp.where(upper, flipped(owner), owner)

    far = place + 2 * core - 1
    has_far = jnp.logical_and(far >= 0, far < blocks)
    crosses = jnp.logical_or(
        jnp.logical_and(place == blocks // 2 - 1, core == 1),
        jnp.logical_and(place == blocks // 2, core == 0),
    )
    sides = (
        (far, jnp.where(crosses, flipped(member), member)),
        (place + 1 - 2 * core, member),
    )

    def each_peer(body):
        lax.fori_loop(
            1, width, lambda _, code: (body(lax.rem(code, 8)), lax.div(code, 8))[1], jnp.int32(FAR_FIRST)
        )

    spot, middle = lax.rem(place, blocks // 2), blocks // 4
    waits = jnp.logical_or(jnp.logical_and(core == 1, spot != middle - 1), spot == middle)
    greets_far = jnp.logical_and(has_far, jnp.logical_not(waits))
    waits_far = jnp.logical_and(has_far, waits)

    barrier = pltpu.get_barrier_semaphore()

    @pl.when(greets_far)
    def _():
        pl.semaphore_signal(barrier, inc=1, device_id=sides[FAR], device_id_type=MESH)

    each_peer(
        lambda r: pl.semaphore_signal(
            barrier, inc=1, device_id=(place, peer(r)), device_id_type=MESH
        )
    )
    pl.semaphore_signal(barrier, inc=1, device_id=sides[CORE], device_id_type=MESH)

    per_slot = block // CHUNK

    def piece(c):
        return slice(c * CHUNK, (c + 1) * CHUNK)

    def columns(owner, h):
        return pl.ds(pl.multiple_of((heads_of(owner) * 2 + h) * HEAD_DIM, HEAD_DIM), HEAD_DIM)

    def token_rows(owner):
        return pl.ds(pl.multiple_of(owner * rows, rows), rows)

    def landing(a, h):
        if a == Q:
            return q_buf.at[h]
        if a == G:
            return g_buf.at[h]
        return (k_buf if a == K else v_buf).at[h, OWN]

    def arrived(a, h, r):
        return first_recv.at[(K, V).index(a), r] if h == 0 and a in (K, V) else in_recv.at[a, h]

    def in_place(a, h):
        return landing(a, h).at[token_rows(member)]

    def wait_bytes(ref, sem):
        pltpu.make_async_copy(ref, ref, sem).wait()

    def in_copy(a, h, r):
        return pltpu.make_async_remote_copy(
            src_ref=inputs[a].at[:, columns(peer(r), h)],
            dst_ref=in_place(a, h),
            send_sem=in_send.at[0],
            recv_sem=arrived(a, h, r),
            device_id=(place, peer(r)),
            device_id_type=MESH,
        )

    def in_own(a, h):
        return pltpu.make_async_copy(
            inputs[a].at[:, columns(member, h)], in_place(a, h), arrived(a, h, 0)
        )

    def send_in(a, h):
        each_peer(lambda r: in_copy(a, h, r).start())

    def wait_in(a, h):
        wait_bytes(landing(a, h), in_recv.at[a, h])

    def halo(a, h, side, part=slice(None)):
        buf, i = (k_buf, 0) if a == K else (v_buf, 1)
        return pltpu.make_async_remote_copy(
            src_ref=buf.at[h, OWN, part],
            dst_ref=buf.at[h, side, part],
            send_sem=halo_send.at[side],
            recv_sem=halo_recv.at[i, h, side],
            device_id=sides[side],
            device_id_type=MESH,
        )

    def edge(i, h, side):
        return pltpu.make_async_remote_copy(
            src_ref=edge_out.at[i, h, side],
            dst_ref=edge_in.at[i, h, side],
            send_sem=edge_send.at[side],
            recv_sem=edge_recv.at[i, h, side],
            device_id=sides[side],
            device_id_type=MESH,
        )

    def if_there(side, action):
        if side == FAR:
            pl.when(has_far)(action)
        else:
            action()

    def start_halo(a, h):
        for side in (FAR, CORE):
            if_there(side, halo(a, h, side).start)

    results = (o_buf, dq_buf, dk_buf, dv_buf)

    def out_copy(i, h, r):
        return pltpu.make_async_remote_copy(
            src_ref=results[i].at[h, token_rows(peer(r))],
            dst_ref=outputs[i].at[:, columns(member, h)],
            send_sem=out_send.at[0],
            recv_sem=out_recv.at[i],
            device_id=(place, peer(r)),
            device_id_type=MESH,
        )

    def out_own(i, h):
        return pltpu.make_async_copy(
            results[i].at[h, token_rows(member)],
            outputs[i].at[:, columns(member, h)],
            out_recv.at[i],
        )

    def send_out(i, h):
        each_peer(lambda r: out_copy(i, h, r).start())
        out_own(i, h).start()

    order = ((K, 0), (V, 0), (Q, 0), (K, 1), (G, 0), (V, 1), (Q, 1), (G, 1))
    for a, h in order:
        in_own(a, h).start()

    pl.semaphore_wait(barrier, width + waits_far.astype(jnp.int32))

    @pl.when(waits_far)
    def _():
        pl.semaphore_signal(near, inc=1, device_id=sides[FAR], device_id_type=MESH)

    for a, h in order:
        send_in(a, h)

    @pl.when(jnp.logical_not(has_far))
    def _():
        k_buf[:, FAR] = jnp.zeros_like(k_buf[:, FAR])
        v_buf[:, FAR] = jnp.zeros_like(v_buf[:, FAR])
        edge_in[:, :, FAR] = jnp.zeros_like(edge_in[:, :, FAR])

    def score_piece(c):
        return slice(c * SCORE_CHUNK, (c + 1) * SCORE_CHUNK)

    def slot_scores(h, slot, query_t):
        best = jnp.full((8, block), -jnp.inf, jnp.float32)
        for c in range(block // SCORE_CHUNK):
            part = dot(k_buf[h, slot, score_piece(c)], query_t)
            scores[slot, score_piece(c)] = part
            best = jnp.maximum(best, jnp.max(part.reshape(SCORE_CHUNK // 8, 8, block), axis=0))
        if slot == FAR:
            best = jnp.where(has_far, best, -jnp.inf)
        return best

    def slot_weights(h, slot, top):
        if slot == FAR:
            top = jnp.where(has_far, top, jnp.float32(1e30))
        total = jnp.zeros((8, block), jnp.float32)
        acc = jnp.zeros((HEAD_DIM, block), jnp.float32)
        for c in range(block // SCORE_CHUNK):
            raised = jnp.exp2(scores[slot, score_piece(c)] * LOG2_SCALE - top)
            total = total + jnp.sum(raised.reshape(SCORE_CHUNK // 8, 8, block), axis=0)
            low = raised.astype(jnp.bfloat16)
            weights[slot, score_piece(c)] = low
            acc = acc + dot(v_buf[h, slot, score_piece(c)].T, low)
        return total, acc

    def slot_grads(h, slot, query, grad, grad_t, row_dot, dk_ref, dv_ref):
        acc = jnp.zeros((HEAD_DIM, block), jnp.float32)
        for c in range(per_slot):
            low = weights[slot, piece(c)]
            grad_probs = dot(v_buf[h, slot, piece(c)], grad_t)
            grad_scores = (low.astype(jnp.float32) * (grad_probs - row_dot)).astype(jnp.bfloat16)
            dv_ref[piece(c)] = dot(low, grad).astype(dv_ref.dtype)
            dk_ref[piece(c)] = dot(grad_scores, query).astype(dk_ref.dtype)
            acc = acc + dot(k_buf[h, slot, piece(c)].T, grad_scores)
        if slot != OWN:
            for i in range(2):
                if_there(slot, edge(i, h, slot).start)
        return acc

    def finish_keys(h):
        for i, (own, buf, scale) in enumerate(((own_dk, dk_buf, SCALE), (own_dv, dv_buf, 1.0))):
            for side in (CORE, FAR):
                if_there(
                    side, lambda: wait_bytes(edge_in.at[i, h, side], edge_recv.at[i, h, side])
                )
            total = (
                own[h]
                + edge_in[i, h, 0].astype(jnp.float32)
                + edge_in[i, h, 1].astype(jnp.float32)
            )
            buf[h] = (total * scale).astype(jnp.bfloat16)
            send_out(DK + i, h)

    def forward(a, h):
        wait_in(a, h)
        start_halo(a, h)

    def forward_pieces(a):
        def step(r):
            part = token_rows(source(r))
            wait_bytes(landing(a, 0).at[part], arrived(a, 0, r))
            for side in (FAR, CORE):
                if_there(side, halo(a, 0, side, part).start)

        step(jnp.int32(0))
        each_peer(step)

    def wait_halo(a, h, side):
        if_there(side, halo(a, h, side).wait_recv)

    @pl.when(greets_far)
    def _():
        pl.semaphore_wait(near, 1)

    forward_pieces(K)
    forward_pieces(V)
    for h in range(2):
        wait_in(Q, h)
        query = q_buf[h]
        query_t = query.T
        best = slot_scores(h, OWN, query_t)
        for slot in (CORE, FAR):
            wait_halo(K, h, slot)
            best = jnp.maximum(best, slot_scores(h, slot, query_t))
        top = jnp.max(best, axis=0, keepdims=True) * LOG2_SCALE
        total, acc = slot_weights(h, OWN, top)
        for slot in (CORE, FAR):
            if h == 0 and slot == FAR:
                forward(K, 1)
            wait_halo(V, h, slot)
            more, term = slot_weights(h, slot, top)
            total, acc = total + more, acc + term
        inverse = 1.0 / jnp.sum(total, axis=0, keepdims=True)
        attended_t = (acc * inverse).astype(jnp.bfloat16)
        o_buf[h] = attended_t.T
        send_out(O, h)
        wait_in(G, h)
        grad_t = (g_buf[h].T.astype(jnp.float32) * inverse).astype(jnp.bfloat16)
        row_dot = jnp.sum(
            grad_t.astype(jnp.float32) * attended_t.astype(jnp.float32), axis=0, keepdims=True
        )
        grad = grad_t.T
        acc = None
        for slot in (CORE, FAR) if h == 0 else (FAR, CORE):
            term = slot_grads(
                h, slot, query, grad, grad_t, row_dot, edge_out.at[0, h, slot], edge_out.at[1, h, slot]
            )
            if acc is None:
                acc = term
                if h == 0:
                    forward(V, 1)
                else:
                    finish_keys(0)
            else:
                acc = acc + term
        acc = acc + slot_grads(h, OWN, query, grad, grad_t, row_dot, own_dk.at[h], own_dv.at[h])
        dq_buf[h] = (acc * SCALE).astype(jnp.bfloat16).T
        send_out(DQ, h)
    one_side, to_others = edge_out.at[:, :, 0], edge_out.at[:, :, :, pl.ds(0, (width - 1) * rows)]
    wait_bytes(to_others, in_send.at[0])
    for side in (FAR, CORE):
        if_there(side, lambda: wait_bytes(one_side, halo_send.at[side]))
    finish_keys(1)

    for side in (FAR, CORE):
        if_there(side, lambda: wait_bytes(one_side, edge_send.at[side]))
    wait_bytes(to_others, out_send.at[0])
    for i in range(4):
        wait_bytes(outputs[i], out_recv.at[i])


def hand_over(*refs):
    sources, targets, done = refs[:4], refs[4:8], refs[8]
    count = done.shape[1]
    rows = sources[0].shape[0] // count
    copies = [
        pltpu.make_async_copy(
            sources[i].at[pl.ds(j * rows, rows)], targets[i].at[pl.ds(j * rows, rows)], done.at[i, j]
        )
        for i in range(4)
        for j in range(count)
    ]
    for copy in copies:
        copy.start()
    for copy in copies:
        copy.wait()


def local(query_in, key_in, value_in, out_grad):
    width = lax.axis_size("uly")
    rows, _ = query_in.shape
    block = rows * width
    heads = HEADS // width
    low, full = jnp.bfloat16, jnp.float32
    dma = pltpu.SemaphoreType.DMA
    whole = pl.BlockSpec(memory_space=pl.ANY)
    query_in, key_in, value_in, out_grad = (
        pltpu.with_memory_space_constraint(array, pltpu.HBM)
        for array in (query_in, key_in, value_in, out_grad)
    )
    results = pl.pallas_call(
        kernel,
        in_specs=[whole] * 4,
        out_specs=[whole] * 4,
        out_shape=[pltpu.VMEM(query_in.shape, low)] * 4,
        scratch_shapes=[
            pltpu.VMEM((heads, block, HEAD_DIM), low),
            pltpu.VMEM((heads, block, HEAD_DIM), low),
            pltpu.VMEM((heads, 3, block, HEAD_DIM), low),
            pltpu.VMEM((heads, 3, block, HEAD_DIM), low),
            pltpu.VMEM((3, block, block), full),
            pltpu.VMEM((3, block, block), low),
            pltpu.VMEM((heads, block, HEAD_DIM), low),
            pltpu.VMEM((heads, block, HEAD_DIM), low),
            pltpu.VMEM((heads, block, HEAD_DIM), low),
            pltpu.VMEM((heads, block, HEAD_DIM), low),
            pltpu.VMEM((heads, block, HEAD_DIM), full),
            pltpu.VMEM((heads, block, HEAD_DIM), full),
            pltpu.VMEM((2, heads, 2, block, HEAD_DIM), low),
            pltpu.VMEM((2, heads, 2, block, HEAD_DIM), low),
            dma((1,)),
            dma((4, heads)),
            dma((2, width)),
            dma((2,)),
            dma((2, heads, 2)),
            dma((2,)),
            dma((2, heads, 2)),
            dma((1,)),
            dma((4,)),
            pltpu.SemaphoreType.REGULAR,
        ],
        compiler_params=pltpu.CompilerParams(
            collective_id=0, has_side_effects=True, vmem_limit_bytes=44 * 2**20
        ),
        cost_estimate=pl.CostEstimate(
            flops=12 * heads * 3 * block * block * HEAD_DIM,
            bytes_accessed=16 * rows * HEADS * HEAD_DIM,
            transcendentals=heads * 3 * block * block,
        ),
    )(query_in, key_in, value_in, out_grad)
    return pl.pallas_call(
        hand_over,
        in_specs=[whole] * 4,
        out_specs=[whole] * 4,
        out_shape=[jax.ShapeDtypeStruct(query_in.shape, low)] * 4,
        scratch_shapes=[dma((4, 1))],
    )(*(pltpu.with_memory_space_constraint(result, pltpu.VMEM) for result in results))


def solution(mesh):
    spec = P(("blk", "uly"), None)
    return jax.shard_map(
        local,
        mesh=mesh,
        in_specs=(spec,) * 4,
        out_specs=(spec,) * 4,
        check_vma=False,
    )
```
